32 devices in a mesh: dp: 8 (over z, y), seq: 4 (over x, core).
Axes of the slice: x: 2, y: 2, z: 4, core: 2. Of those that a mesh axis runs over, the one named last changes fastest.
Arguments:
- tokens: bfloat16 [48, 1024, 576], P('dp', 'seq'), may hold values from -6 to 6
- cotangent: bfloat16 [48, 1024, 576], P('dp', 'seq'), may hold values from -6 to 6
- attn_gain: bfloat16 [576], P(('dp', 'seq')), may hold values from 0.25 to 1.75
- query_weight: bfloat16 [331776], P(('dp', 'seq')), may hold values from -0.375 to 0.375
- key_weight: bfloat16 [110592], P(('dp', 'seq')), may hold values from -0.375 to 0.375
- value_weight: bfloat16 [110592], P(('dp', 'seq')), may hold values from -0.25 to 0.25
- out_weight: bfloat16 [331776], P(('dp', 'seq')), may hold values from -1.5 to 1.5
- mlp_gain: bfloat16 [576], P(('dp', 'seq')), may hold values from 0.25 to 1.75
- gate_weight: bfloat16 [884736], P(('dp', 'seq')), may hold values from -0.25 to 0.25
- up_weight: bfloat16 [884736], P(('dp', 'seq')), may hold values from -0.25 to 0.25
- down_weight: bfloat16 [884736], P(('dp', 'seq')), may hold values from -0.3125 to 0.3125
Outputs:
- output: bfloat16 [48, 1024, 576], P('dp', 'seq')
- tokens_grad: bfloat16 [48, 1024, 576], P('dp', 'seq')
- attn_gain_grad: float32 [576], P(('dp', 'seq'))
- query_grad: float32 [331776], P(('dp', 'seq'))
- key_grad: float32 [110592], P(('dp', 'seq'))
- value_grad: float32 [110592], P(('dp', 'seq'))
- out_grad: float32 [331776], P(('dp', 'seq'))
- mlp_gain_grad: float32 [576], P(('dp', 'seq'))
- gate_grad: float32 [884736], P(('dp', 'seq'))
- up_grad: float32 [884736], P(('dp', 'seq'))
- down_grad: float32 [884736], P(('dp', 'seq'))
The draws below stay inside these ranges and needn't reach their ends.
All inputs are finite; a program needn't handle non-finite values.
Results may differ from the reference program's by a relative error of at most 0.015.
The reference program's roundings to bfloat16 on the way count: a program that leaves them out, or rounds other values in their place, can miss the bound.
Values may be sent and summed in bfloat16 or wider, within the bound.
No kernel may reach another device: no remote copies, remote signals or barrier semaphores. Data moves between devices by JAX's collectives and lax.ppermute only.
A program may use at most 192 MiB of HBM per device.

```python
import jax
import jax.numpy as jnp
from jax import lax

D = 576
HEADS = 9
KVH = 3
HD = 64
FF = 1536
LENGTH = 1024
SEQS = 48
GAIN_FLAT = 576
Q_FLAT = 331776
KV_FLAT = 110592
FF_FLAT = 884736


def level_of(rng, shape, split, low, high):
    loudness, own = 1.0, jax.random.fold_in(rng, 6)
    for dim, shards_of in split:
        draws = jnp.exp(jax.random.uniform(jax.random.fold_in(own, dim), (shards_of,), jnp.float32, low / len(split), high / len(split)))
        loudness = loudness * jnp.repeat(draws, shape[dim] // shards_of).reshape([-1 if axis == dim else 1 for axis in range(len(shape))])
    return loudness


def centred(key, extent, deviation, most, shards=(), held_as=jnp.bfloat16):
    level = level_of(key, extent, shards, -0.22, 0.18) if shards else 1.0
    entries = jax.random.normal(key, extent, jnp.float32) * deviation * level
    return jnp.minimum(jnp.maximum(entries, -most), most).astype(held_as)


def setup_inputs(seed: int = 0) -> dict:
    seeds = jax.random.split(jax.random.key(seed), 12)
    return {
        "tokens": centred(seeds[0], (SEQS, LENGTH, D), 1.0, 6.0, ((0, 8), (1, 4))),
        "cotangent": centred(seeds[1], (SEQS, LENGTH, D), 1.0, 6.0, ((0, 8), (1, 4))),
        "attn_gain": jnp.clip(1.0 + 0.15 * jax.random.normal(seeds[2], (GAIN_FLAT,), jnp.float32), 0.25, 1.75).astype(jnp.bfloat16),
        "query_weight": centred(seeds[3], (Q_FLAT,), (D // 2) ** -0.5, 0.375, ((0, 32),)),
        "key_weight": centred(seeds[4], (KV_FLAT,), (D // 2) ** -0.5, 0.375, ((0, 32),)),
        "value_weight": centred(seeds[5], (KV_FLAT,), D ** -0.5, 0.25, ((0, 32),)),
        "out_weight": centred(seeds[6], (Q_FLAT,), (D // 32) ** -0.5, 1.5, ((0, 32),)),
        "mlp_gain": jnp.clip(1.0 + 0.15 * jax.random.normal(seeds[7], (GAIN_FLAT,), jnp.float32), 0.25, 1.75).astype(jnp.bfloat16),
        "gate_weight": centred(seeds[8], (FF_FLAT,), D ** -0.5, 0.25, ((0, 32),)),
        "up_weight": centred(seeds[9], (FF_FLAT,), D ** -0.5, 0.25, ((0, 32),)),
        "down_weight": centred(seeds[10], (FF_FLAT,), (FF // 4) ** -0.5, 0.3125, ((0, 32),)),
    }


@jax.custom_vjp
def low(v):
    return lax.optimization_barrier(v.astype(jnp.bfloat16)).astype(jnp.float32)

@jax.custom_vjp
def low_back(v):
    return v

def low_keep(v):
    return (low(v), None)

def low_pass(kept, grad):
    return (grad,)

def back_keep(v):
    return (v, None)

def back_low(kept, grad):
    return (low(grad),)
low.defvjp(low_keep, low_pass)
low_back.defvjp(back_keep, back_low)
epsilon = 1e-05
rope_base = 100000.0

def matmul(left, right):
    return jnp.dot(left, right, precision=lax.Precision.HIGHEST)

def rms_norm(values, gain):
    return values * lax.rsqrt(lax.optimization_barrier(jnp.mean(values * values, axis=-1, keepdims=True)) + epsilon) * gain

def rotate(values, cosine, sine):
    half_dim = values.shape[-1] // 2
    first = values[..., :half_dim]
    second = values[..., half_dim:]
    return jnp.concatenate([first * cosine - second * sine, second * cosine + first * sine], axis=-1)

def attend_group(blocks):
    queries, key_rows, value_rows = blocks
    length = key_rows.shape[0]
    scores = low_back(jnp.einsum('gqd,kd->gqk', queries, key_rows, precision=lax.Precision.HIGHEST)) * HD ** (-0.5)
    causal = jnp.arange(length)[:, None] >= jnp.arange(length)[None, :]
    scores = jnp.where(causal[None], scores, -1e+30)
    biggest = lax.optimization_barrier(jnp.max(scores, axis=-1, keepdims=True))
    weights = jnp.exp(scores - biggest)
    probs = weights / lax.optimization_barrier(jnp.sum(weights, axis=-1, keepdims=True))
    return jnp.einsum('gqk,kd->gqd', low(probs), value_rows, precision=lax.Precision.HIGHEST)

def layer_forward(tokens, attn_gain, query_weight, key_weight, value_weight, out_weight, mlp_gain, gate_weight, up_weight, down_weight):
    length, width = tokens.shape
    kv_width = KVH * HD
    group = HEADS // KVH
    w_query = query_weight[:width * width].reshape(width, width)
    w_key = key_weight[:width * kv_width].reshape(width, kv_width)
    w_value = value_weight[:width * kv_width].reshape(width, kv_width)
    w_out = out_weight[:width * width].reshape(width, width)
    w_gate = gate_weight[:width * FF].reshape(width, FF)
    w_up = up_weight[:width * FF].reshape(width, FF)
    w_down = down_weight[:FF * width].reshape(FF, width)
    positions = jnp.arange(length).astype(tokens.dtype)
    freqs = rope_base ** (-2.0 * jnp.arange(HD // 2).astype(tokens.dtype) / HD)
    angles = positions[:, None] * freqs[None, :]
    cosine = jnp.cos(angles)[:, None, :]
    sine = jnp.sin(angles)[:, None, :]
    normed = low(rms_norm(tokens, attn_gain[:width]))
    queries = low(rotate(low_back(matmul(normed, w_query)).reshape(length, HEADS, HD), cosine, sine))
    key_rows = low(rotate(low_back(matmul(normed, w_key)).reshape(length, KVH, HD), cosine, sine))
    value_rows = low(low_back(matmul(normed, w_value))).reshape(length, KVH, HD)
    grouped = queries.reshape(length, KVH, group, HD).transpose(1, 2, 0, 3)
    mixed = lax.map(jax.checkpoint(attend_group), (grouped, key_rows.transpose(1, 0, 2), value_rows.transpose(1, 0, 2)))
    attended = low(low_back(mixed.transpose(2, 0, 1, 3).reshape(length, width)))
    resid = tokens + low_back(matmul(attended, w_out))
    normed_two = low(rms_norm(resid, mlp_gain[:width]))
    gate_pre = low_back(matmul(normed_two, w_gate))
    up_pre = low_back(matmul(normed_two, w_up))
    hidden = low(jax.nn.silu(gate_pre) * up_pre)
    return resid + low_back(matmul(hidden, w_down))

def reference(tokens, cotangent, attn_gain, query_weight, key_weight, value_weight, out_weight, mlp_gain, gate_weight, up_weight, down_weight):
    params = tuple((weight.astype(jnp.float32) for weight in (attn_gain, query_weight, key_weight, value_weight, out_weight, mlp_gain, gate_weight, up_weight, down_weight)))

    def one_sequence(totals, pair):
        sequence, sequence_cot = pair
        result, pullback = jax.vjp(layer_forward, sequence, *params)
        grads = pullback(sequence_cot)
        summed = tuple((total + grad for total, grad in zip(totals, grads[1:])))
        return (summed, (result.astype(jnp.bfloat16), grads[0].astype(jnp.bfloat16)))
    start = tuple((jnp.zeros_like(weight) for weight in params))
    totals, (outputs, token_grads) = lax.scan(one_sequence, start, (tokens.astype(jnp.float32), cotangent.astype(jnp.float32)))
    return (outputs, token_grads, totals[0], totals[1], totals[2], totals[3], totals[4], totals[5], totals[6], totals[7], totals[8])
```

```python
import functools

import jax
import jax.numpy as jnp
from jax import lax
from jax.experimental import pallas as pl
from jax.experimental.pallas import tpu as pltpu
from jax.sharding import PartitionSpec as P

HEADS = 9
KVH = 3
HD = 64
FF = 1536
GROUP = HEADS // KVH
KVD = KVH * HD
FF_BLOCK = 512

epsilon = 1e-05
rope_base = 100000.0
MASKED = -1e30
VMEM_LIMIT = 60 * 1024 * 1024
AXES = ("dp", "seq")


def nn(left, right):
    return jnp.dot(left, right, preferred_element_type=jnp.float32)


def nt(left, right):
    return lax.dot_general(
        left, right, (((1,), (1,)), ((), ())), preferred_element_type=jnp.float32
    )


def tn(left, right):
    return lax.dot_general(
        left, right, (((0,), (0,)), ((), ())), preferred_element_type=jnp.float32
    )


def whole(shape):
    return pl.BlockSpec(shape, lambda *_: (0,) * len(shape), pipeline_mode=pl.Buffered(1))


def params(count):
    return pltpu.CompilerParams(
        dimension_semantics=("arbitrary",) * count, vmem_limit_bytes=VMEM_LIMIT
    )


def unflatten(flat_ref, tmp_ref, out_ref, rows, width):
    if width % 128 == 0:
        count = width // 128
        for j in range(count):
            piece = flat_ref[pl.ds(j, rows, stride=count), :]
            out_ref[:, 128 * j : 128 * (j + 1)] = piece.astype(out_ref.dtype)
        return
    count = 2 * width // 128
    mid = count // 2
    left = lax.broadcasted_iota(jnp.int32, (rows // 2, 128), 1) < 64
    turned = [
        pltpu.roll(flat_ref[pl.ds(mid + j, rows // 2, stride=count), :], 64, 1)
        for j in range(mid + 1)
    ]
    for j in range(mid + 1):
        odd = jnp.where(left, turned[j], turned[j + 1]) if j < mid else turned[j]
        tmp_ref[pl.ds(0, rows // 2, stride=2), :] = flat_ref[pl.ds(j, rows // 2, stride=count), :]
        tmp_ref[pl.ds(1, rows // 2, stride=2), :] = odd
        size = min(128, width - 128 * j)
        out_ref[:, 128 * j : 128 * j + size] = tmp_ref[:rows, :size].astype(out_ref.dtype)


def flatten(grad_ref, tmp_ref, flat_ref, rows, width):
    if width % 128 == 0:
        count = width // 128
        for j in range(count):
            flat_ref[pl.ds(j, rows, stride=count), :] = grad_ref[:, 128 * j : 128 * (j + 1)]
        return
    count = 2 * width // 128
    mid = count // 2
    left = lax.broadcasted_iota(jnp.int32, (rows // 2, 128), 1) < 64
    before = None
    for j in range(mid + 1):
        size = min(128, width - 128 * j)
        tmp_ref[:rows, :size] = grad_ref[:, 128 * j : 128 * j + size]
        even = tmp_ref[pl.ds(0, rows // 2, stride=2), :]
        turned = pltpu.roll(tmp_ref[pl.ds(1, rows // 2, stride=2), :], 64, 1)
        if j < mid:
            flat_ref[pl.ds(j, rows // 2, stride=count), :] = even
            if j == 0:
                first = turned
        else:
            flat_ref[pl.ds(mid, rows // 2, stride=count), :] = jnp.where(left, even, first)
        if j:
            flat_ref[pl.ds(mid + j, rows // 2, stride=count), :] = jnp.where(left, before, turned)
        before = turned


def project_rows(x_ref, gain, wt_ref, cos_ref, sin_ref, q_ref, kv_ref):
    width = x_ref.shape[-1]
    x = x_ref[0].astype(jnp.float32)
    inverse = lax.rsqrt(jnp.mean(x * x, axis=-1, keepdims=True) + epsilon)
    normed = (x * inverse * gain).astype(jnp.bfloat16)
    out = nt(wt_ref[...], normed)
    cosine, sine = cos_ref[...], sin_ref[...]
    half = HD // 2
    for head in range(HEADS + KVH):
        a = out[head * HD : head * HD + half]
        b = out[head * HD + half : (head + 1) * HD]
        first = (a * cosine - b * sine).astype(jnp.bfloat16)
        second = (b * cosine + a * sine).astype(jnp.bfloat16)
        if head < HEADS:
            q_ref[0, head * HD : head * HD + half, :] = first
            q_ref[0, head * HD + half : (head + 1) * HD, :] = second
        else:
            kv_ref[0, 0, head - HEADS, :half, :] = first
            kv_ref[0, 0, head - HEADS, half:, :] = second
    for head in range(KVH):
        start = width + KVD + head * HD
        kv_ref[0, 1, head] = out[start : start + HD].astype(jnp.bfloat16)


def project_kernel(
    x_ref, gain_ref, wq_ref, wk_ref, wv_ref, cos_ref, sin_ref, q_ref, kv_ref, wt_ref
):
    width = x_ref.shape[-1]

    @pl.when(pl.program_id(0) == 0)
    def _():
        wt_ref[:width, :] = wq_ref[...].T
        wt_ref[width : width + KVD, :] = wk_ref[...].T
        wt_ref[width + KVD :, :] = wv_ref[...].T

    project_rows(x_ref, gain_ref[...], wt_ref, cos_ref, sin_ref, q_ref, kv_ref)


def early_places(width, devices):
    places, start = [], 0
    for columns in (width, KVD, KVD):
        count = width * columns // 128 // devices
        places.append((columns, start, count))
        start += count
    return places, start


def project_packed_kernel(
    me_ref, x_ref, packed_ref, cos_ref, sin_ref, q_ref, kv_ref, wt_ref, gains_ref,
    flat_ref, tmp_ref, weight_ref,
):
    width = x_ref.shape[-1]
    devices = packed_ref.shape[0]
    places, gain_row = early_places(width, devices)
    share = width // devices

    @pl.when(pl.program_id(0) == 0)
    def _():
        me = me_ref[0]
        top = 0
        for columns, start, count in places:
            for d in range(devices):
                flat_ref[d * count : (d + 1) * count, :] = packed_ref[
                    d ^ me, start : start + count, :
                ].astype(jnp.float32)
            unflatten(flat_ref, tmp_ref, weight_ref, width, columns)
            wt_ref[top : top + columns, :] = weight_ref[:, :columns].T
            top += columns
        for d in range(devices):
            for which in range(2):
                row = gain_row + which
                gains_ref[which : which + 1, d * share : (d + 1) * share] = packed_ref[
                    d ^ me, row : row + 1, :share
                ].astype(jnp.float32)

    project_rows(x_ref, gains_ref[0:1, :], wt_ref, cos_ref, sin_ref, q_ref, kv_ref)


def gather_keys(own, other, span):
    return jnp.concatenate([own[:, span:], own[:, :span], other], axis=1)


def stack_heads(ref, offset, span):
    return jnp.concatenate(
        [ref[0, h * HD : (h + 1) * HD, offset : offset + span] for h in range(GROUP)], axis=1
    )


def causal_mask(span):
    key = lax.broadcasted_iota(jnp.int32, (span, span), 0)
    query = lax.broadcasted_iota(jnp.int32, (span, span), 1)
    return jnp.concatenate([key <= query] * GROUP, axis=1)


def parts_of(kind, span):
    if kind == 0:
        return ((span, 0, 4 * span), (0, span, span))
    return ((span, 0, 3 * span), (0, span, 2 * span))


def masked_scores(keys, queries, mask, span):
    scores = nn(keys, queries)
    top = jnp.where(mask, scores[:span], MASKED)
    if keys.shape[0] == span:
        return top
    return jnp.concatenate([top, scores[span:]], axis=0)


def attend_kernel(kind_ref, q_ref, kv_ref, other_ref, o_ref, lse_ref):
    span = q_ref.shape[-1] // 2
    keys = gather_keys(kv_ref[0, 0, 0], other_ref[0, 0, 0], span).T
    values_t = gather_keys(kv_ref[0, 1, 0], other_ref[0, 1, 0], span)
    mask = causal_mask(span)

    def run(kind):
        for offset, start, count in parts_of(kind, span):
            queries = stack_heads(q_ref, offset, span) * HD ** (-0.5)
            scores = masked_scores(keys[start : start + count], queries, mask, span)
            biggest = jnp.max(scores, axis=0, keepdims=True)
            weights = jnp.exp(scores - biggest)
            totals = jnp.sum(weights, axis=0, keepdims=True)
            mixed = nn(values_t[:, start : start + count], weights.astype(jnp.bfloat16))
            mixed = (mixed / totals).astype(jnp.bfloat16)
            lse = biggest + jnp.log(totals)
            for h in range(GROUP):
                lanes = slice(h * span, (h + 1) * span)
                o_ref[0, h * HD : (h + 1) * HD, offset : offset + span] = mixed[:, lanes]
                lse_ref[0, 0, h : h + 1, offset : offset + span] = lse[:, lanes]

    for kind in range(2):
        pl.when(kind_ref[0] == kind)(functools.partial(run, kind))


def attend_back_kernel(
    kind_ref, q_ref, kv_ref, other_ref, do_ref, lse_ref, cos_ref, sin_ref,
    dq_ref, own_ref, away_ref, dk_ref, dv_ref,
):
    span = q_ref.shape[-1] // 2
    half = HD // 2
    scale = HD ** (-0.5)
    keys_t = gather_keys(kv_ref[0, 0, 0], other_ref[0, 0, 0], span)
    values_t = gather_keys(kv_ref[0, 1, 0], other_ref[0, 1, 0], span)
    keys = keys_t.T
    values = values_t.T
    mask = causal_mask(span)

    def run(kind):
        for index, (offset, start, count) in enumerate(parts_of(kind, span)):
            rows = slice(start, start + count)
            queries = stack_heads(q_ref, offset, span) * scale
            grads = stack_heads(do_ref, offset, span)
            lse = jnp.concatenate(
                [lse_ref[0, 0, h : h + 1, offset : offset + span] for h in range(GROUP)], axis=1
            )
            probs = jnp.exp(masked_scores(keys[rows], queries, mask, span) - lse)
            prob_grads = nn(values[rows], grads)
            delta = jnp.sum(prob_grads * probs, axis=0, keepdims=True)
            score_grads = (probs * (prob_grads - delta)).astype(jnp.bfloat16)
            dv = nt(probs.astype(jnp.bfloat16), grads)
            dk = nt(score_grads, queries)
            if index == 0:
                dk_ref[rows, :] = dk
                dv_ref[rows, :] = dv
                if count < 4 * span:
                    dk_ref[count:, :] = jnp.zeros((4 * span - count, HD), jnp.float32)
                    dv_ref[count:, :] = jnp.zeros((4 * span - count, HD), jnp.float32)
            else:
                dk_ref[rows, :] += dk
                dv_ref[rows, :] += dv
            dq = nn(keys_t[:, rows], score_grads) * scale
            place = 0 if offset else span
            cosine = cos_ref[:, place : place + span]
            sine = sin_ref[:, place : place + span]
            for h in range(GROUP):
                a = dq[:half, h * span : (h + 1) * span]
                b = dq[half:, h * span : (h + 1) * span]
                lanes = slice(offset, offset + span)
                dq_ref[0, h * HD : h * HD + half, lanes] = (a * cosine + b * sine).astype(
                    jnp.bfloat16
                )
                dq_ref[0, h * HD + half : (h + 1) * HD, lanes] = (
                    b * cosine - a * sine
                ).astype(jnp.bfloat16)

    for kind in range(2):
        pl.when(kind_ref[0] == kind)(functools.partial(run, kind))

    def put(ref, which, grads_t):
        ref[0, which, 0] = grads_t.astype(ref.dtype)

    dk_t = dk_ref[...].T
    a, b = dk_t[:half], dk_t[half:]
    cosine, sine = cos_ref[...], sin_ref[...]
    dk_t = jnp.concatenate([a * cosine + b * sine, b * cosine - a * sine], axis=0)
    dv_t = dv_ref[...].T
    for which, grads_t in ((0, dk_t), (1, dv_t)):
        put(
            own_ref,
            which,
            jnp.concatenate([grads_t[:, span : 2 * span], grads_t[:, :span]], axis=1),
        )
        put(away_ref, which, grads_t[:, 2 * span :])


def mlp_kernel(
    o_ref, x_ref, cot_ref, gain_ref, wo_ref, wg_ref, wu_ref, wd_ref,
    out_ref, do_ref, dx_ref, dwo_ref, dwg_ref, dwu_ref, dwd_ref, dgain_ref,
):
    def put(ref, index, value):
        first = pl.program_id(0) == 0

        @pl.when(first)
        def _():
            ref[index] = value

        @pl.when(jnp.logical_not(first))
        def _():
            ref[index] += value

    mixed_t = o_ref[0]
    x1 = x_ref[0].astype(jnp.float32) + nn(mixed_t.T, wo_ref[...])
    inverse = lax.rsqrt(jnp.mean(x1 * x1, axis=-1, keepdims=True) + epsilon)
    normed_f = x1 * inverse
    gain = gain_ref[...]
    normed = (normed_f * gain).astype(jnp.bfloat16)
    normed_t = normed.T
    cot = cot_ref[0]
    result = x1
    dnormed = jnp.zeros(x1.shape, jnp.float32)
    for start in range(0, FF, FF_BLOCK):
        cols = slice(start, start + FF_BLOCK)
        gate = nn(normed, wg_ref[:, cols])
        up = nn(normed, wu_ref[:, cols])
        sigma = jax.nn.sigmoid(gate)
        silu = gate * sigma
        hidden = (silu * up).astype(jnp.bfloat16)
        result = result + nn(hidden, wd_ref[cols, :])
        dhidden = nt(cot, wd_ref[cols, :])
        dgate = (dhidden * up * (sigma * (1.0 + gate * (1.0 - sigma)))).astype(jnp.bfloat16)
        dup = (dhidden * silu).astype(jnp.bfloat16)
        dnormed = dnormed + nt(dgate, wg_ref[:, cols]) + nt(dup, wu_ref[:, cols])
        put(dwg_ref, (slice(None), cols), nn(normed_t, dgate))
        put(dwu_ref, (slice(None), cols), nn(normed_t, dup))
        put(dwd_ref, (cols, slice(None)), tn(hidden, cot))
    out_ref[0] = result.astype(jnp.bfloat16)
    put(dgain_ref, ..., jnp.sum(dnormed * normed_f, axis=0, keepdims=True))
    scaled = dnormed * gain
    dx = cot.astype(jnp.float32) + inverse * (
        scaled - normed_f * jnp.mean(scaled * normed_f, axis=-1, keepdims=True)
    )
    dx_ref[0] = dx
    dab = dx.astype(jnp.bfloat16)
    put(dwo_ref, ..., nn(mixed_t, dab))
    do_ref[0] = nt(wo_ref[...], dab).astype(jnp.bfloat16)


def late_places(width, devices):
    places, start = [], 0
    for rows, columns in ((width, width), (width, FF), (width, FF), (FF, width)):
        count = rows * columns // 128 // devices
        places.append((rows, columns, start, count))
        start += -(-(count + 1) // 16) * 16
    return places, start


def mlp_packed_kernel(
    o_ref, x_ref, cot_ref, gain_ref, packed_ref, out_ref, do_ref, dx_ref, sums_ref,
    wo_ref, wg_ref, wu_ref, wd_ref, dwo_ref, dwg_ref, dwu_ref, dwd_ref, dgain_ref,
    flat_ref, tmp_ref, stage_ref, sems,
):
    width = x_ref.shape[-1]
    devices = packed_ref.shape[0]
    places, total = late_places(width, devices)
    tops = [place[2] for place in places] + [total]
    sizes = [after - before for before, after in zip(tops, tops[1:])]
    step = pl.program_id(0)

    def arrival(i):
        return pltpu.make_async_copy(
            packed_ref.at[:, tops[i] : tops[i + 1], :],
            stage_ref.at[i % 2, :, : sizes[i], :],
            sems.at[i % 2],
        )

    def departure(i):
        return pltpu.make_async_copy(
            stage_ref.at[i % 2, :, : sizes[i], :],
            sums_ref.at[:, tops[i] : tops[i + 1], :],
            sems.at[i % 2],
        )

    @pl.when(step == 0)
    def _():
        arrival(0).start()
        arrival(1).start()
        for i, (ref, (rows, columns, _, count)) in enumerate(
            zip((wo_ref, wg_ref, wu_ref, wd_ref), places)
        ):
            arrival(i).wait()
            for d in range(devices):
                flat_ref[d * count : (d + 1) * count, :] = stage_ref[i % 2, d, :count, :].astype(
                    jnp.float32
                )
            if i + 2 < len(places):
                arrival(i + 2).start()
            unflatten(flat_ref, tmp_ref, ref, rows, columns)

    mlp_kernel(
        o_ref, x_ref, cot_ref, gain_ref, wo_ref, wg_ref, wu_ref, wd_ref,
        out_ref, do_ref, dx_ref, dwo_ref, dwg_ref, dwu_ref, dwd_ref, dgain_ref,
    )

    @pl.when(step == pl.num_programs(0) - 1)
    def _():
        share = width // devices
        for i, (ref, (rows, columns, _, count)) in enumerate(
            zip((dwo_ref, dwg_ref, dwu_ref, dwd_ref), places)
        ):
            flatten(ref, tmp_ref, flat_ref, rows, columns)
            if i >= 2:
                departure(i - 2).wait()
            for d in range(devices):
                block = flat_ref[d * count : (d + 1) * count, :]
                if i == 0:
                    tail = jnp.concatenate(
                        [
                            dgain_ref[0:1, d * share : (d + 1) * share],
                            jnp.zeros((1, 128 - share), jnp.float32),
                        ],
                        axis=1,
                    )
                    block = jnp.concatenate(
                        [block, tail, jnp.zeros((sizes[0] - count - 1, 128), jnp.float32)], axis=0
                    )
                    stage_ref[i % 2, d, : sizes[0], :] = block.astype(jnp.bfloat16)
                else:
                    stage_ref[i % 2, d, :count, :] = block.astype(jnp.bfloat16)
            departure(i).start()
        departure(len(places) - 2).wait()
        departure(len(places) - 1).wait()


def final_rows(
    dq_ref, own_ref, here_ref, x_ref, dx_ref, gain_ref, wt_ref, grad_ref, dgain_ref, acc_ref
):
    span, width = x_ref.shape[1:]
    step = pl.program_id(0)
    dkv = own_ref[0].astype(jnp.float32) + here_ref[0].astype(jnp.float32)
    d_t = jnp.concatenate([dq_ref[0], dkv.astype(jnp.bfloat16).reshape(2 * KVD, span)], axis=0)
    x = x_ref[0].astype(jnp.float32)
    inverse = lax.rsqrt(jnp.mean(x * x, axis=-1, keepdims=True) + epsilon)
    normed_f = x * inverse
    gain = gain_ref[...]
    normed = (normed_f * gain).astype(jnp.bfloat16)
    grads = nn(d_t, normed)
    dnormed = tn(d_t, wt_ref[...])
    dgain = jnp.sum(dnormed * normed_f, axis=0, keepdims=True)

    @pl.when(step == 0)
    def _():
        acc_ref[...] = grads
        dgain_ref[...] = dgain

    @pl.when(step > 0)
    def _():
        acc_ref[...] += grads
        dgain_ref[...] += dgain

    scaled = dnormed * gain
    grad_ref[0] = (
        dx_ref[0]
        + inverse * (scaled - normed_f * jnp.mean(scaled * normed_f, axis=-1, keepdims=True))
    ).astype(jnp.bfloat16)


def final_kernel(
    dq_ref, own_ref, here_ref, x_ref, dx_ref, gain_ref, wt_ref,
    grad_ref, dwq_ref, dwk_ref, dwv_ref, dgain_ref, acc_ref,
):
    width = x_ref.shape[-1]
    final_rows(
        dq_ref, own_ref, here_ref, x_ref, dx_ref, gain_ref, wt_ref, grad_ref, dgain_ref, acc_ref
    )

    @pl.when(pl.program_id(0) == pl.num_programs(0) - 1)
    def _():
        dwq_ref[...] = acc_ref[:width, :].T
        dwk_ref[...] = acc_ref[width : width + KVD, :].T
        dwv_ref[...] = acc_ref[width + KVD :, :].T


def final_packed_kernel(
    dq_ref, own_ref, here_ref, x_ref, dx_ref, gain_ref, wt_ref,
    grad_ref, sums_ref, dgain_ref, acc_ref, flat_ref, tmp_ref, weight_ref, block_ref,
):
    width = x_ref.shape[-1]
    devices = sums_ref.shape[0]
    places, gain_row = early_places(width, devices)
    share = width // devices
    final_rows(
        dq_ref, own_ref, here_ref, x_ref, dx_ref, gain_ref, wt_ref, grad_ref, dgain_ref, acc_ref
    )

    @pl.when(pl.program_id(0) == pl.num_programs(0) - 1)
    def _():
        top = 0
        for which, (columns, _, _) in enumerate(places):
            weight_ref[:, :columns] = acc_ref[top : top + columns, :].T
            flatten(weight_ref, tmp_ref, flat_ref.at[which], width, columns)
            top += columns
        block_ref[...] = jnp.zeros(block_ref.shape, jnp.float32)
        for d in range(devices):
            for which, (_, start, count) in enumerate(places):
                block_ref[start : start + count, :] = flat_ref[
                    which, d * count : (d + 1) * count, :
                ]
            block_ref[gain_row : gain_row + 1, :share] = dgain_ref[
                0:1, d * share : (d + 1) * share
            ]
            sums_ref[d] = block_ref[...].astype(jnp.bfloat16)


def struct(shape, dtype):
    return jax.ShapeDtypeStruct(shape, dtype)


def per_seq(*shape):
    return pl.BlockSpec((1, *shape), lambda s, *_: (s,) + (0,) * len(shape))


def project(x, gain, w_query, w_key, w_value, cosine, sine):
    seqs, rows, width = x.shape
    return pl.pallas_call(
        project_kernel,
        grid=(seqs,),
        in_specs=[
            per_seq(rows, width),
            whole((1, width)),
            whole((width, width)),
            whole((width, KVD)),
            whole((width, KVD)),
            whole((HD // 2, rows)),
            whole((HD // 2, rows)),
        ],
        out_specs=[
            per_seq(width, rows),
            per_seq(2, KVH, HD, rows),
            whole((width + 2 * KVD, width)),
        ],
        out_shape=[
            struct((seqs, width, rows), jnp.bfloat16),
            struct((seqs, 2, KVH, HD, rows), jnp.bfloat16),
            struct((width + 2 * KVD, width), jnp.bfloat16),
        ],
        compiler_params=params(1),
        name="project",
    )(x, gain, w_query, w_key, w_value, cosine, sine)


def project_packed(me, x, packed, cosine, sine):
    seqs, rows, width = x.shape
    return pl.pallas_call(
        project_packed_kernel,
        grid=(seqs,),
        in_specs=[
            pl.BlockSpec(memory_space=pltpu.SMEM),
            per_seq(rows, width),
            whole(packed.shape),
            whole((HD // 2, rows)),
            whole((HD // 2, rows)),
        ],
        out_specs=[
            per_seq(width, rows),
            per_seq(2, KVH, HD, rows),
            whole((width + 2 * KVD, width)),
            whole((8, width)),
        ],
        out_shape=[
            struct((seqs, width, rows), jnp.bfloat16),
            struct((seqs, 2, KVH, HD, rows), jnp.bfloat16),
            struct((width + 2 * KVD, width), jnp.bfloat16),
            struct((8, width), jnp.float32),
        ],
        scratch_shapes=[
            pltpu.VMEM((width * width // 128, 128), jnp.float32),
            pltpu.VMEM((width, 128), jnp.float32),
            pltpu.VMEM((width, width), jnp.bfloat16),
        ],
        compiler_params=params(1),
        name="project",
    )(me, x, packed, cosine, sine)


def per_group(rows):
    heads = pl.BlockSpec((1, GROUP * HD, rows), lambda s, g: (s, g, 0))
    pairs = pl.BlockSpec((1, 2, 1, HD, rows), lambda s, g: (s, 0, g, 0, 0))
    stats = pl.BlockSpec((1, 1, 8, rows), lambda s, g: (s, g, 0, 0))
    kind = pl.BlockSpec(memory_space=pltpu.SMEM)
    return heads, pairs, stats, kind


def attend(kind, queries, pairs, other):
    seqs, width, rows = queries.shape
    heads, kv, stats, smem = per_group(rows)
    return pl.pallas_call(
        attend_kernel,
        grid=(seqs, KVH),
        in_specs=[smem, heads, kv, kv],
        out_specs=[heads, stats],
        out_shape=[
            struct(queries.shape, jnp.bfloat16),
            struct((seqs, KVH, 8, rows), jnp.float32),
        ],
        compiler_params=params(2),
        name="attend",
    )(kind, queries, pairs, other)


def attend_back(kind, queries, pairs, other, grads, lse, cosine, sine):
    seqs, width, rows = queries.shape
    heads, kv, stats, smem = per_group(rows)
    return pl.pallas_call(
        attend_back_kernel,
        grid=(seqs, KVH),
        in_specs=[smem, heads, kv, kv, heads, stats]
        + [whole((HD // 2, 2 * rows)), whole((HD // 2, 2 * rows))],
        out_specs=[heads, kv, kv],
        out_shape=[
            struct(queries.shape, jnp.bfloat16),
            struct(pairs.shape, jnp.float32),
            struct(pairs.shape, jnp.float32),
        ],
        scratch_shapes=[
            pltpu.VMEM((2 * rows, HD), jnp.float32),
            pltpu.VMEM((2 * rows, HD), jnp.float32),
        ],
        compiler_params=params(2),
        name="attend_back",
    )(kind, queries, pairs, other, grads, lse, cosine, sine)


def mlp(mixed, x, cot, gain, w_out, w_gate, w_up, w_down):
    seqs, rows, width = x.shape
    weights = [whole((width, width)), whole((width, FF)), whole((width, FF)), whole((FF, width))]
    return pl.pallas_call(
        mlp_kernel,
        grid=(seqs,),
        in_specs=[per_seq(width, rows), per_seq(rows, width), per_seq(rows, width)]
        + [whole((1, width))]
        + weights,
        out_specs=[per_seq(rows, width), per_seq(width, rows), per_seq(rows, width)]
        + weights
        + [whole((1, width))],
        out_shape=[
            struct((seqs, rows, width), jnp.bfloat16),
            struct((seqs, width, rows), jnp.bfloat16),
            struct((seqs, rows, width), jnp.float32),
            struct((width, width), jnp.float32),
            struct((width, FF), jnp.float32),
            struct((width, FF), jnp.float32),
            struct((FF, width), jnp.float32),
            struct((1, width), jnp.float32),
        ],
        compiler_params=params(1),
        name="mlp",
    )(mixed, x, cot, gain, w_out, w_gate, w_up, w_down)


def mlp_packed(mixed, x, cot, gain, packed):
    seqs, rows, width = x.shape
    shapes = [(width, width), (width, FF), (width, FF), (FF, width)]
    places, _ = late_places(width, packed.shape[0])
    return pl.pallas_call(
        mlp_packed_kernel,
        grid=(seqs,),
        in_specs=[per_seq(width, rows), per_seq(rows, width), per_seq(rows, width)]
        + [whole((1, width)), pl.BlockSpec(memory_space=pl.ANY)],
        out_specs=[per_seq(rows, width), per_seq(width, rows), per_seq(rows, width)]
        + [pl.BlockSpec(memory_space=pl.ANY)],
        out_shape=[
            struct((seqs, rows, width), jnp.bfloat16),
            struct((seqs, width, rows), jnp.bfloat16),
            struct((seqs, rows, width), jnp.float32),
            struct(packed.shape, jnp.bfloat16),
        ],
        scratch_shapes=[pltpu.VMEM(shape, jnp.bfloat16) for shape in shapes]
        + [pltpu.VMEM(shape, jnp.float32) for shape in shapes]
        + [
            pltpu.VMEM((1, width), jnp.float32),
            pltpu.VMEM((width * FF // 128, 128), jnp.float32),
            pltpu.VMEM((FF, 128), jnp.float32),
            pltpu.VMEM((2, packed.shape[0], places[2][2] - places[1][2], 128), jnp.bfloat16),
            pltpu.SemaphoreType.DMA((2,)),
        ],
        compiler_params=params(1),
        name="mlp",
    )(mixed, x, cot, gain, packed)


def final_packed(dq, own, here, x, dx, gain, weights_t, devices, height):
    seqs, rows, width = x.shape
    flat = width * width // 128
    return pl.pallas_call(
        final_packed_kernel,
        grid=(seqs,),
        in_specs=[
            per_seq(width, rows),
            per_seq(2, KVH, HD, rows),
            per_seq(2, KVH, HD, rows),
            per_seq(rows, width),
            per_seq(rows, width),
            whole((1, width)),
            whole((width + 2 * KVD, width)),
        ],
        out_specs=[per_seq(rows, width), whole((devices, height, 128))],
        out_shape=[
            struct((seqs, rows, width), jnp.bfloat16),
            struct((devices, height, 128), jnp.bfloat16),
        ],
        scratch_shapes=[
            pltpu.VMEM((1, width), jnp.float32),
            pltpu.VMEM((width + 2 * KVD, width), jnp.float32),
            pltpu.VMEM((3, flat, 128), jnp.float32),
            pltpu.VMEM((width, 128), jnp.float32),
            pltpu.VMEM((width, width), jnp.float32),
            pltpu.VMEM((height, 128), jnp.float32),
        ],
        compiler_params=params(1),
        name="final",
    )(dq, own, here, x, dx, gain, weights_t)


def final(dq, own, here, x, dx, gain, weights_t):
    seqs, rows, width = x.shape
    return pl.pallas_call(
        final_kernel,
        grid=(seqs,),
        in_specs=[
            per_seq(width, rows),
            per_seq(2, KVH, HD, rows),
            per_seq(2, KVH, HD, rows),
            per_seq(rows, width),
            per_seq(rows, width),
            whole((1, width)),
            whole((width + 2 * KVD, width)),
        ],
        out_specs=[
            per_seq(rows, width),
            whole((width, width)),
            whole((width, KVD)),
            whole((width, KVD)),
            whole((1, width)),
        ],
        out_shape=[
            struct((seqs, rows, width), jnp.bfloat16),
            struct((width, width), jnp.float32),
            struct((width, KVD), jnp.float32),
            struct((width, KVD), jnp.float32),
            struct((1, width), jnp.float32),
        ],
        scratch_shapes=[pltpu.VMEM((width + 2 * KVD, width), jnp.float32)],
        compiler_params=params(1),
        name="final",
    )(dq, own, here, x, dx, gain, weights_t)


def gather(shards, devices):
    sizes = [shard.shape[0] for shard in shards]
    joined = jnp.concatenate(shards)
    padded = -(-joined.shape[0] // 2048) * 2048
    joined = jnp.pad(joined, (0, padded - joined.shape[0])).reshape(-1, 128)
    every = lax.all_gather(joined, AXES, axis=0, tiled=True).reshape(devices, padded)
    found, start = [], 0
    for size in sizes:
        found.append(every[:, start : start + size].reshape(devices * size))
        start += size
    return found


def scatter_sum(grads, sizes, devices):
    pieces = [
        jnp.pad(grad.reshape(-1), (0, devices * size - grad.size)).reshape(devices, size)
        for grad, size in zip(grads, sizes)
    ]
    joined = jnp.concatenate(pieces, axis=1)
    total = sum(sizes)
    padded = -(-total // 2048) * 2048
    joined = jnp.pad(joined, ((0, 0), (0, padded - total))).astype(jnp.bfloat16)
    joined = joined.reshape(devices * padded // 128, 128)
    owned = lax.psum_scatter(joined, AXES, scatter_dimension=0, tiled=True)
    owned = owned.reshape(-1).astype(jnp.float32)
    found, start = [], 0
    for size in sizes:
        found.append(owned[start : start + size])
        start += size
    return found


def bit_swap(array, bit, devices):
    return lax.ppermute(array, AXES, [(i, i ^ bit) for i in range(devices)])


def split_bits(devices):
    bits = [1 << i for i in range(devices.bit_length() - 1)]
    return bits[0], bits[1], bits[2], bits[3:]


def gather_doubling(block, devices):
    core, first, second, rest = split_bits(devices)
    held = block[None]
    for bit in reversed(rest):
        held = jnp.concatenate([held, bit_swap(held, bit, devices)])
    cut = block.shape[0] // 2
    upper, lower = held[:, :cut], held[:, cut:]
    upper_other = bit_swap(upper, second, devices)
    lower_other = bit_swap(lower, first, devices)
    upper = jnp.stack([upper, upper_other])
    lower = jnp.stack([lower, lower_other])
    upper_other = bit_swap(upper, first, devices)
    lower_other = bit_swap(lower, second, devices)
    upper = jnp.stack([upper, upper_other])
    lower = jnp.stack([lower, lower_other])
    held = jnp.concatenate([upper, lower.swapaxes(0, 1)], axis=3)
    held = jnp.stack([held, bit_swap(held, core, devices)])
    count = len(rest)
    held = held.reshape((2,) * (3 + count) + block.shape)
    order = tuple(reversed(range(3 + count)))
    return held.transpose(order + (3 + count, 4 + count)).reshape((devices,) + block.shape)


def halve(array, axis, side):
    keep = lax.dynamic_index_in_dim(array, side, axis, keepdims=False)
    send = lax.dynamic_index_in_dim(array, 1 - side, axis, keepdims=False)
    return keep, send


def sum_halving(blocks, me, devices):
    core, first, second, rest = split_bits(devices)
    side = {bit: (me // bit) % 2 for bit in [core, first, second] + rest}
    rows = blocks.shape[1]
    count = len(rest)
    cut = rows // 2

    def step(array, axis, bit):
        keep, send = halve(array, axis, side[bit])
        came = bit_swap(send.astype(jnp.bfloat16), bit, devices)
        return keep.astype(jnp.float32) + came.astype(jnp.float32)

    held = blocks.reshape((2,) * (count + 3) + (rows, 128))
    held = step(held, count + 2, core)
    upper, lower = held[..., :cut, :], held[..., cut:, :]
    upper = step(upper, count + 1, first)
    lower = step(lower, count, second)
    upper = step(upper, count, second)
    lower = step(lower, count, first)
    held = jnp.concatenate([upper, lower], axis=-2)
    for bit in rest:
        count -= 1
        held = step(held, count, bit)
    return held


def body(
    tokens, cotangent, attn_gain, query_weight, key_weight, value_weight, out_weight,
    mlp_gain, gate_weight, up_weight, down_weight,
):
    seqs_here, span, width = tokens.shape
    n_seq = lax.axis_size("seq")
    devices = lax.axis_size("dp") * n_seq
    mine = lax.axis_index("seq")
    keep = seqs_here // 2
    across = [(i, n_seq - 1 - i) for i in range(n_seq)]
    beside = [(i, i ^ 1) for i in range(n_seq)]
    low_half = mine < n_seq // 2

    def exchange(blocks):
        kept = lax.dynamic_slice_in_dim(blocks, jnp.where(low_half, 0, keep), keep, 0)
        sent = lax.dynamic_slice_in_dim(blocks, jnp.where(low_half, keep, 0), keep, 0)
        came = lax.ppermute(sent, "seq", across)
        low = jnp.where(low_half, kept, came)
        high = jnp.where(low_half, came, kept)
        return jnp.concatenate([low, high], axis=1)

    def restore(blocks):
        low, high = blocks[:, :span], blocks[:, span:]
        kept = jnp.where(low_half, low, high)
        came = lax.ppermute(jnp.where(low_half, high, low), "seq", across)
        front = jnp.where(low_half, kept, came)
        back = jnp.where(low_half, came, kept)
        return jnp.concatenate([front, back], axis=0)

    shards = (query_weight, key_weight, value_weight, out_weight, gate_weight, up_weight, down_weight)
    packed = devices & (devices - 1) == 0 and devices >= 16 and width % devices == 0
    packed = packed and all(shard.shape[0] % 128 == 0 for shard in shards)
    packed = packed and attn_gain.shape[0] * devices == width

    me = lax.axis_index(AXES)
    x = exchange(tokens)
    freqs = rope_base ** (-2.0 * jnp.arange(HD // 2).astype(jnp.float32) / HD)
    low_block = jnp.minimum(mine, n_seq - 1 - mine)
    other_low = jnp.minimum(mine ^ 1, n_seq - 1 - (mine ^ 1))
    blocks = jnp.stack([n_seq - 1 - low_block, low_block, other_low, n_seq - 1 - other_low])
    positions = (blocks[:, None] * span + jnp.arange(span)[None, :]).reshape(-1)
    angles = freqs[:, None] * positions.astype(jnp.float32)[None, :]
    cosine, sine = jnp.cos(angles), jnp.sin(angles)

    def low_high(table):
        return jnp.concatenate([table[:, span : 2 * span], table[:, :span]], axis=1)

    kind = low_block.astype(jnp.int32).reshape(1)

    if packed:
        places, gain_row = early_places(width, devices)
        height = -(-(gain_row + 2) // 16) * 16
        gains = jnp.pad(jnp.stack([attn_gain, mlp_gain]), ((0, 0), (0, 128 - attn_gain.shape[0])))
        rows = [shard.reshape(-1, 128) for shard in shards[:3]] + [gains]
        block = jnp.concatenate(rows)
        block = jnp.pad(block, ((0, height - block.shape[0]), (0, 0)))
        early = gather_doubling(block, devices)
        late_spots, late_height = late_places(width, devices)
        tops = [spot[2] for spot in late_spots] + [late_height]
        rows = [
            jnp.pad(shard.reshape(-1, 128), ((0, after - before - spot[3]), (0, 0)))
            for shard, spot, before, after in zip(shards[3:], late_spots, tops, tops[1:])
        ]
        late = lax.all_gather(jnp.concatenate(rows), AXES, axis=0, tiled=True)
        late = late.reshape(devices, late_height, 128)
        queries, pairs, weights_t, gains = project_packed(
            me.astype(jnp.int32).reshape(1), x, early, low_high(cosine), low_high(sine)
        )
        attn_scale, mlp_scale = gains[0:1], gains[1:2]
    else:
        early = gather((attn_gain, query_weight, key_weight, value_weight), devices)
        late = gather((mlp_gain, out_weight, gate_weight, up_weight, down_weight), devices)
        attn_scale = early[0][:width].astype(jnp.float32).reshape(1, width)
        mlp_scale = late[0][:width].astype(jnp.float32).reshape(1, width)
        w_query = early[1][: width * width].reshape(width, width)
        w_key = early[2][: width * KVD].reshape(width, KVD)
        w_value = early[3][: width * KVD].reshape(width, KVD)
        w_out = late[1][: width * width].reshape(width, width)
        w_gate = late[2][: width * FF].reshape(width, FF)
        w_up = late[3][: width * FF].reshape(width, FF)
        w_down = late[4][: FF * width].reshape(FF, width)
        queries, pairs, weights_t = project(
            x, attn_scale, w_query, w_key, w_value, low_high(cosine), low_high(sine)
        )

    other = lax.ppermute(pairs, "seq", beside)
    cotangent, _ = lax.optimization_barrier((cotangent, queries))
    cot = exchange(cotangent)
    mixed, lse = attend(kind, queries, pairs, other)
    if packed:
        out, dmixed, dx, late_sums = mlp_packed(mixed, x, cot, mlp_scale, late)
        owned = sum_halving(late_sums, me, devices)
        out_sum, gate_sum, up_sum, down_sum = [
            owned[start : start + count].reshape(-1) for _, _, start, count in late_spots
        ]
        mlp_sum = owned[late_spots[0][3], : mlp_gain.shape[0]]
    else:
        out, dmixed, dx, grad_out, grad_gate, grad_up, grad_down, grad_mlp_scale = mlp(
            mixed, x, cot, mlp_scale, w_out, w_gate, w_up, w_down
        )
        mlp_sum, out_sum, gate_sum, up_sum, down_sum = scatter_sum(
            (grad_mlp_scale, grad_out, grad_gate, grad_up, grad_down),
            [a.shape[0] for a in (mlp_gain,) + shards[3:]],
            devices,
        )
    output = restore(out)
    dq, own, away = attend_back(kind, queries, pairs, other, dmixed, lse, cosine, sine)
    here = lax.ppermute(away, "seq", beside)
    if packed:
        dtokens, early_sums = final_packed(
            dq, own, here, x, dx, attn_scale, weights_t, devices, height
        )
        owned = sum_halving(early_sums, me, devices)
        query_sum, key_sum, value_sum = [
            owned[start : start + count].reshape(-1) for _, start, count in places
        ]
        attn_sum = owned[gain_row, : attn_gain.shape[0]]
    else:
        dtokens, grad_query, grad_key, grad_value, grad_attn_scale = final(
            dq, own, here, x, dx, attn_scale, weights_t
        )
        attn_sum, query_sum, key_sum, value_sum = scatter_sum(
            (grad_attn_scale, grad_query, grad_key, grad_value),
            [a.shape[0] for a in (attn_gain,) + shards[:3]],
            devices,
        )
    tokens_grad = restore(dtokens)
    return (
        output, tokens_grad, attn_sum, query_sum, key_sum, value_sum,
        out_sum, mlp_sum, gate_sum, up_sum, down_sum,
    )


def solution(mesh):
    rows = P("dp", "seq", None)
    flat = P(("dp", "seq"))
    return jax.shard_map(
        body,
        mesh=mesh,
        in_specs=(rows, rows) + (flat,) * 9,
        out_specs=(rows, rows) + (flat,) * 9,
        check_vma=False,
    )
```

```python
import functools

import jax
import jax.numpy as jnp
from jax import lax
from jax.experimental import pallas as pl
from jax.experimental.pallas import tpu as pltpu
from jax.sharding import PartitionSpec as P

HEADS = 9
KVH = 3
HD = 64
FF = 1536
GROUP = HEADS // KVH
KVD = KVH * HD
FF_BLOCK = 768

epsilon = 1e-05
rope_base = 100000.0
MASKED = -1e30
VMEM_LIMIT = 60 * 1024 * 1024
AXES = ("dp", "seq")


def nn(left, right):
    return jnp.dot(left, right, preferred_element_type=jnp.float32)


def nt(left, right):
    return lax.dot_general(
        left, right, (((1,), (1,)), ((), ())), preferred_element_type=jnp.float32
    )


def tn(left, right):
    return lax.dot_general(
        left, right, (((0,), (0,)), ((), ())), preferred_element_type=jnp.float32
    )


def cost(micros):
    return pl.CostEstimate(flops=int(micros * 5e8), bytes_accessed=int(micros * 1e6), transcendentals=0)


def whole(shape):
    return pl.BlockSpec(shape, lambda *_: (0,) * len(shape), pipeline_mode=pl.Buffered(1))


def params(count):
    return pltpu.CompilerParams(
        dimension_semantics=("arbitrary",) * count, vmem_limit_bytes=VMEM_LIMIT
    )


def unflatten(flat_ref, tmp_ref, out_ref, rows, width, left_column=0):
    if width % 128 == 0:
        count = width // 128
        for j in range(count):
            piece = flat_ref[pl.ds(j, rows, stride=count), :]
            place = left_column + 128 * j
            out_ref[:, place : place + 128] = piece.astype(out_ref.dtype)
        return
    count = 2 * width // 128
    mid = count // 2
    left = lax.broadcasted_iota(jnp.int32, (rows // 2, 128), 1) < 64
    turned = [
        pltpu.roll(flat_ref[pl.ds(mid + j, rows // 2, stride=count), :], 64, 1)
        for j in range(mid + 1)
    ]
    for j in range(mid + 1):
        odd = jnp.where(left, turned[j], turned[j + 1]) if j < mid else turned[j]
        tmp_ref[pl.ds(0, rows // 2, stride=2), :] = flat_ref[pl.ds(j, rows // 2, stride=count), :]
        tmp_ref[pl.ds(1, rows // 2, stride=2), :] = odd
        size = min(128, width - 128 * j)
        place = left_column + 128 * j
        out_ref[:, place : place + size] = tmp_ref[:rows, :size].astype(out_ref.dtype)


def flatten(grad_ref, tmp_ref, flat_ref, rows, width, left_column=0):
    if width % 128 == 0:
        count = width // 128
        for j in range(count):
            flat_ref[pl.ds(j, rows, stride=count), :] = grad_ref[
                :, left_column + 128 * j : left_column + 128 * (j + 1)
            ]
        return
    count = 2 * width // 128
    mid = count // 2
    left = lax.broadcasted_iota(jnp.int32, (rows // 2, 128), 1) < 64
    before = None
    for j in range(mid + 1):
        size = min(128, width - 128 * j)
        place = left_column + 128 * j
        tmp_ref[:rows, :size] = grad_ref[:, place : place + size]
        even = tmp_ref[pl.ds(0, rows // 2, stride=2), :]
        turned = pltpu.roll(tmp_ref[pl.ds(1, rows // 2, stride=2), :], 64, 1)
        if j < mid:
            flat_ref[pl.ds(j, rows // 2, stride=count), :] = even
            if j == 0:
                first = turned
        else:
            flat_ref[pl.ds(mid, rows // 2, stride=count), :] = jnp.where(left, even, first)
        if j:
            flat_ref[pl.ds(mid + j, rows // 2, stride=count), :] = jnp.where(left, before, turned)
        before = turned


def join(info_ref, own_ref, came_ref):
    own_low = info_ref[2] == 1
    own, came = own_ref[0].astype(jnp.float32), came_ref[0].astype(jnp.float32)
    low = jnp.where(own_low, own, came)
    high = jnp.where(own_low, came, own)
    return jnp.concatenate([low, high], axis=1)


def part(info_ref, values, own_ref, sent_ref):
    span = own_ref.shape[-1]
    own_low = info_ref[2] == 1
    low, high = values[:, :span], values[:, span:]
    own_ref[0] = jnp.where(own_low, low, high).astype(own_ref.dtype)
    sent_ref[0] = jnp.where(own_low, high, low).astype(sent_ref.dtype)


def normalise(x):
    inverse = lax.rsqrt(jnp.mean(x * x, axis=0, keepdims=True) + epsilon)
    return inverse, x * inverse


def project_rows(x, gain, wt_ref, cos_ref, sin_ref, q_ref, kv_ref):
    _, normed_f = normalise(x)
    out = nn(wt_ref[...], (normed_f * gain).astype(jnp.bfloat16))
    cosine, sine = cos_ref[...], sin_ref[...]
    half = HD // 2
    for head in range(HEADS + KVH):
        start = head * HD if head < KVH else 2 * KVD + (head - KVH) * HD
        a = out[start : start + half]
        b = out[start + half : start + HD]
        first = (a * cosine - b * sine).astype(jnp.bfloat16)
        second = (b * cosine + a * sine).astype(jnp.bfloat16)
        if head < KVH:
            kv_ref[0, 0, head, :half, :] = first
            kv_ref[0, 0, head, half:, :] = second
        else:
            spot = (head - KVH) * HD
            q_ref[0, spot : spot + half, :] = first
            q_ref[0, spot + half : spot + HD, :] = second
    for head in range(KVH):
        start = KVD + head * HD
        kv_ref[0, 1, head] = out[start : start + HD].astype(jnp.bfloat16)


def project_kernel(
    info_ref, own_ref, came_ref, gains_ref, wq_ref, wk_ref, wv_ref, cos_ref, sin_ref,
    q_ref, kv_ref, weights_ref, wt_ref,
):
    @pl.when(pl.program_id(0) == 0)
    def _():
        weights_ref[:, :KVD] = wk_ref[...]
        weights_ref[:, KVD : 2 * KVD] = wv_ref[...]
        weights_ref[:, 2 * KVD :] = wq_ref[...]
        wt_ref[...] = weights_ref[...].T

    x = join(info_ref, own_ref, came_ref)
    project_rows(x, gains_ref[:, 0:1], wt_ref, cos_ref, sin_ref, q_ref, kv_ref)


def early_places(width, devices):
    places, start = [], 0
    for columns, left in ((KVD, 0), (KVD, KVD), (width, 2 * KVD)):
        count = width * columns // 128 // devices
        places.append((columns, left, start, count))
        start += count
    return places, start


def project_packed_kernel(
    order, info_ref, own_ref, came_ref, packed_ref, cos_ref, sin_ref,
    q_ref, kv_ref, weights_ref, gains_ref, wt_ref, flat_ref, tmp_ref, row_ref,
):
    width = own_ref.shape[1]
    devices = packed_ref.shape[0]
    places, gain_row = early_places(width, devices)
    share = width // devices

    @pl.when(pl.program_id(0) == 0)
    def _():
        spots = []
        for d in range(devices):
            away = d ^ info_ref[1]
            spot = 0
            for bit in order:
                spot = spot * 2 + (away // bit) % 2
            spots.append(spot)
        for columns, left, start, count in places:
            for d in range(devices):
                flat_ref[d * count : (d + 1) * count, :] = packed_ref[
                    spots[d], start : start + count, :
                ].astype(jnp.float32)
            unflatten(flat_ref, tmp_ref, weights_ref, width, columns, left)
        wt_ref[...] = weights_ref[...].T
        row_ref[...] = jnp.zeros(row_ref.shape, jnp.float32)
        for d in range(devices):
            row_ref[0:2, d * share : (d + 1) * share] = packed_ref[
                spots[d], gain_row : gain_row + 2, :share
            ].astype(jnp.float32)
        gains_ref[...] = row_ref[...].T

    x = join(info_ref, own_ref, came_ref)
    project_rows(x, gains_ref[:, 0:1], wt_ref, cos_ref, sin_ref, q_ref, kv_ref)


def gather_keys(own, other, span):
    return jnp.concatenate([own[:, span:], own[:, :span], other], axis=1)


def stack_heads(ref, offset, span):
    return jnp.concatenate(
        [ref[0, h * HD : (h + 1) * HD, offset : offset + span] for h in range(GROUP)], axis=1
    )


def causal_mask(span):
    key = lax.broadcasted_iota(jnp.int32, (span, span), 0)
    query = lax.broadcasted_iota(jnp.int32, (span, span), 1)
    return jnp.concatenate([key <= query] * GROUP, axis=1)


def parts_of(kind, span):
    if kind == 0:
        return ((span, 0, 4 * span), (0, span, span))
    return ((span, 0, 3 * span), (0, span, 2 * span))


def masked_scores(keys, queries, mask, span):
    scores = nn(keys, queries)
    top = jnp.where(mask, scores[:span], MASKED)
    if keys.shape[0] == span:
        return top
    return jnp.concatenate([top, scores[span:]], axis=0)


def attend_kernel(kind_ref, q_ref, kv_ref, other_ref, o_ref, inverse_ref, weights_ref):
    span = q_ref.shape[-1] // 2
    keys = gather_keys(kv_ref[0, 0, 0], other_ref[0, 0, 0], span).T
    values_t = gather_keys(kv_ref[0, 1, 0], other_ref[0, 1, 0], span)
    mask = causal_mask(span)

    def run(kind):
        top = 0
        for offset, start, count in parts_of(kind, span):
            queries = stack_heads(q_ref, offset, span) * HD ** (-0.5)
            scores = masked_scores(keys[start : start + count], queries, mask, span)
            biggest = jnp.max(scores, axis=0, keepdims=True)
            weights = jnp.exp(scores - biggest)
            inverse = 1.0 / jnp.sum(weights, axis=0, keepdims=True)
            weights = weights.astype(jnp.bfloat16)
            weights_ref[0, 0, top : top + count, :] = weights
            top += count
            mixed = nn(values_t[:, start : start + count], weights)
            mixed = (mixed * inverse).astype(jnp.bfloat16)
            for h in range(GROUP):
                lanes = slice(h * span, (h + 1) * span)
                o_ref[0, h * HD : (h + 1) * HD, offset : offset + span] = mixed[:, lanes]
                inverse_ref[0, 0, h : h + 1, offset : offset + span] = inverse[:, lanes]

    for kind in range(2):
        pl.when(kind_ref[0] == kind)(functools.partial(run, kind))


def attend_back_kernel(
    kind_ref, q_ref, kv_ref, other_ref, do_ref, inverse_ref, weights_ref, cos_ref, sin_ref,
    dq_ref, own_ref, away_ref, dk_ref, dv_ref,
):
    span = q_ref.shape[-1] // 2
    half = HD // 2
    scale = HD ** (-0.5)
    keys_t = gather_keys(kv_ref[0, 0, 0], other_ref[0, 0, 0], span)
    values = gather_keys(kv_ref[0, 1, 0], other_ref[0, 1, 0], span).T

    def run(kind):
        top = 0
        for index, (offset, start, count) in enumerate(parts_of(kind, span)):
            rows = slice(start, start + count)
            queries = stack_heads(q_ref, offset, span) * scale
            inverse = jnp.concatenate(
                [inverse_ref[0, 0, h : h + 1, offset : offset + span] for h in range(GROUP)],
                axis=1,
            )
            grads = stack_heads(do_ref, offset, span).astype(jnp.float32) * inverse
            grads = grads.astype(jnp.bfloat16)
            weights = weights_ref[0, 0, top : top + count, :]
            top += count
            weight_grads = nn(values[rows], grads)
            weights_f = weights.astype(jnp.float32)
            delta = jnp.sum(weight_grads * weights_f, axis=0, keepdims=True) * inverse
            score_grads = (weights_f * (weight_grads - delta)).astype(jnp.bfloat16)
            dv = nt(weights, grads)
            dk = nt(score_grads, queries)
            if index == 0:
                dk_ref[rows, :] = dk
                dv_ref[rows, :] = dv
                if count < 4 * span:
                    dk_ref[count:, :] = jnp.zeros((4 * span - count, HD), jnp.float32)
                    dv_ref[count:, :] = jnp.zeros((4 * span - count, HD), jnp.float32)
            else:
                dk_ref[rows, :] += dk
                dv_ref[rows, :] += dv
            dq = nn(keys_t[:, rows], score_grads) * scale
            place = 0 if offset else span
            cosine = cos_ref[:, place : place + span]
            sine = sin_ref[:, place : place + span]
            for h in range(GROUP):
                a = dq[:half, h * span : (h + 1) * span]
                b = dq[half:, h * span : (h + 1) * span]
                lanes = slice(offset, offset + span)
                dq_ref[0, h * HD : h * HD + half, lanes] = (a * cosine + b * sine).astype(
                    jnp.bfloat16
                )
                dq_ref[0, h * HD + half : (h + 1) * HD, lanes] = (
                    b * cosine - a * sine
                ).astype(jnp.bfloat16)

    for kind in range(2):
        pl.when(kind_ref[0] == kind)(functools.partial(run, kind))

    def put(ref, which, grads_t):
        ref[0, which, 0] = grads_t.astype(ref.dtype)

    dk_t = dk_ref[...].T
    a, b = dk_t[:half], dk_t[half:]
    cosine, sine = cos_ref[...], sin_ref[...]
    dk_t = jnp.concatenate([a * cosine + b * sine, b * cosine - a * sine], axis=0)
    dv_t = dv_ref[...].T
    for which, grads_t in ((0, dk_t), (1, dv_t)):
        put(
            own_ref,
            which,
            jnp.concatenate([grads_t[:, span : 2 * span], grads_t[:, :span]], axis=1),
        )
        put(away_ref, which, grads_t[:, 2 * span :])


def mlp_rows(
    info_ref, o_ref, own_ref, came_ref, cot_ref, cot_came_ref, gains_ref,
    wo_ref, wg_ref, wu_ref, wd_ref, wot_ref, wgt_ref, wut_ref, wdt_ref,
    out_ref, sent_ref, do_ref, dx_ref, dwo_ref, dwg_ref, dwu_ref, dwd_ref, dgain_ref,
):
    def put(ref, index, value):
        first = pl.program_id(0) == 0

        @pl.when(first)
        def _():
            ref[index] = value

        @pl.when(jnp.logical_not(first))
        def _():
            ref[index] += value

    mixed = o_ref[0]
    x1 = join(info_ref, own_ref, came_ref) + nn(wot_ref[...], mixed)
    inverse, normed_f = normalise(x1)
    gain = gains_ref[:, 1:2]
    normed = (normed_f * gain).astype(jnp.bfloat16)
    cot = join(info_ref, cot_ref, cot_came_ref).astype(jnp.bfloat16)
    result = x1
    dnormed = jnp.zeros(x1.shape, jnp.float32)
    for start in range(0, FF, FF_BLOCK):
        cols = slice(start, start + FF_BLOCK)
        gate = nn(wgt_ref[cols, :], normed)
        up = nn(wut_ref[cols, :], normed)
        sigma = jax.nn.sigmoid(gate)
        silu = gate * sigma
        hidden = (silu * up).astype(jnp.bfloat16)
        result = result + nn(wdt_ref[:, cols], hidden)
        dhidden = nn(wd_ref[cols, :], cot)
        dgate = (dhidden * up * (sigma * (1.0 + gate * (1.0 - sigma)))).astype(jnp.bfloat16)
        dup = (dhidden * silu).astype(jnp.bfloat16)
        dnormed = dnormed + nn(wg_ref[:, cols], dgate) + nn(wu_ref[:, cols], dup)
        put(dwg_ref, (slice(None), cols), nt(normed, dgate))
        put(dwu_ref, (slice(None), cols), nt(normed, dup))
        put(dwd_ref, (cols, slice(None)), nt(hidden, cot))
    part(info_ref, result, out_ref, sent_ref)
    put(dgain_ref, ..., jnp.sum(dnormed * normed_f, axis=1, keepdims=True))
    scaled = dnormed * gain
    dx = cot.astype(jnp.float32) + inverse * (
        scaled - normed_f * jnp.mean(scaled * normed_f, axis=0, keepdims=True)
    )
    dx_ref[0] = dx
    dab = dx.astype(jnp.bfloat16)
    put(dwo_ref, ..., nt(mixed, dab))
    do_ref[0] = nn(wo_ref[...], dab).astype(jnp.bfloat16)


def mlp_kernel(*refs):
    info_ref, o_ref, own_ref, came_ref, cot_ref, cot_came_ref, gains_ref, *refs = refs
    weights, refs = refs[:4], refs[4:]
    outs, turned = refs[:-4], refs[-4:]

    @pl.when(pl.program_id(0) == 0)
    def _():
        for ref, other in zip(weights, turned):
            other[...] = ref[...].T

    mlp_rows(
        info_ref, o_ref, own_ref, came_ref, cot_ref, cot_came_ref, gains_ref,
        *weights, *turned, *outs,
    )


def late_places(width, devices):
    places, start = [], 0
    for rows, columns in ((width, width), (width, FF), (width, FF), (FF, width)):
        count = rows * columns // 128 // devices
        places.append((rows, columns, start, count))
        start += -(-(count + 1) // 16) * 16
    return places, start


def mlp_packed_kernel(
    info_ref, o_ref, own_ref, came_ref, cot_ref, cot_came_ref, gains_ref, packed_ref,
    out_ref, sent_ref, do_ref, dx_ref, keep_ref, send_ref,
    wo_ref, wg_ref, wu_ref, wd_ref, wot_ref, wgt_ref, wut_ref, wdt_ref,
    dwo_ref, dwg_ref, dwu_ref, dwd_ref, dgain_ref, flat_ref, tmp_ref, stage_ref, sems,
):
    width = own_ref.shape[1]
    devices = packed_ref.shape[0]
    places, total = late_places(width, devices)
    tops = [place[2] for place in places] + [total]
    sizes = [after - before for before, after in zip(tops, tops[1:])]
    step = pl.program_id(0)

    half = devices // 2
    core = info_ref[1] % 2

    def arrival(i):
        return [
            pltpu.make_async_copy(
                packed_ref.at[side * half : (side + 1) * half, tops[i] : tops[i + 1], :],
                stage_ref.at[i % 2, side, :, : sizes[i], :],
                sems.at[i % 2, side],
            )
            for side in range(2)
        ]

    def departure(i):
        return [
            pltpu.make_async_copy(
                stage_ref.at[i % 2, source, :, : sizes[i], :],
                ref.at[:, tops[i] : tops[i + 1], :],
                sems.at[i % 2, side],
            )
            for side, (ref, source) in enumerate(((keep_ref, core), (send_ref, 1 - core)))
        ]

    def start(copies):
        for copy in copies:
            copy.start()

    def wait(copies):
        for copy in copies:
            copy.wait()

    @pl.when(step == 0)
    def _():
        start(arrival(0))
        start(arrival(1))
        turned = (wot_ref, wgt_ref, wut_ref, wdt_ref)
        for i, (ref, (rows, columns, _, count)) in enumerate(
            zip((wo_ref, wg_ref, wu_ref, wd_ref), places)
        ):
            wait(arrival(i))
            for d in range(devices):
                flat_ref[d * count : (d + 1) * count, :] = stage_ref[
                    i % 2, d // half, d % half, :count, :
                ].astype(jnp.float32)
            if i + 2 < len(places):
                start(arrival(i + 2))
            unflatten(flat_ref, tmp_ref, ref, rows, columns)
            turned[i][...] = ref[...].T

    mlp_rows(
        info_ref, o_ref, own_ref, came_ref, cot_ref, cot_came_ref, gains_ref,
        wo_ref, wg_ref, wu_ref, wd_ref, wot_ref, wgt_ref, wut_ref, wdt_ref,
        out_ref, sent_ref, do_ref, dx_ref, dwo_ref, dwg_ref, dwu_ref, dwd_ref, dgain_ref,
    )

    @pl.when(step == pl.num_programs(0) - 1)
    def _():
        share = width // devices
        dgain = jnp.broadcast_to(dgain_ref[...], (width, 128)).T[0:1]
        for i, (ref, (rows, columns, _, count)) in enumerate(
            zip((dwo_ref, dwg_ref, dwu_ref, dwd_ref), places)
        ):
            flatten(ref, tmp_ref, flat_ref, rows, columns)
            if i >= 2:
                wait(departure(i - 2))
            for d in range(devices):
                block = flat_ref[d * count : (d + 1) * count, :]
                if i == 0:
                    tail = jnp.concatenate(
                        [
                            dgain[:, d * share : (d + 1) * share],
                            jnp.zeros((1, 128 - share), jnp.float32),
                        ],
                        axis=1,
                    )
                    block = jnp.concatenate(
                        [block, tail, jnp.zeros((sizes[0] - count - 1, 128), jnp.float32)], axis=0
                    )
                    stage_ref[i % 2, d % 2, d // 2, : sizes[0], :] = block.astype(jnp.bfloat16)
                else:
                    stage_ref[i % 2, d % 2, d // 2, :count, :] = block.astype(jnp.bfloat16)
            start(departure(i))
        wait(departure(len(places) - 2))
        wait(departure(len(places) - 1))


def final_rows(
    info_ref, dq_ref, kv_ref, own_ref, came_ref, dx_ref, gains_ref, weights_ref, here_refs,
    out_ref, sent_ref, dgain_ref, acc_ref, dkv_ref,
):
    rows = dq_ref.shape[-1]
    step = pl.program_id(0)
    for seq, here_ref in enumerate(here_refs):

        @pl.when(step == seq)
        def _():
            dkv_ref[...] = (kv_ref[0] + here_ref[0].astype(jnp.float32)).astype(jnp.bfloat16)

    d = jnp.concatenate([dkv_ref[...].reshape(2 * KVD, rows), dq_ref[0]], axis=0)
    inverse, normed_f = normalise(join(info_ref, own_ref, came_ref))
    gain = gains_ref[:, 0:1]
    normed = (normed_f * gain).astype(jnp.bfloat16)
    grads = nt(normed, d)
    dnormed = nn(weights_ref[...], d)
    dgain = jnp.sum(dnormed * normed_f, axis=1, keepdims=True)

    @pl.when(step == 0)
    def _():
        acc_ref[...] = grads
        dgain_ref[...] = dgain

    @pl.when(step > 0)
    def _():
        acc_ref[...] += grads
        dgain_ref[...] += dgain

    scaled = dnormed * gain
    dx = dx_ref[0] + inverse * (
        scaled - normed_f * jnp.mean(scaled * normed_f, axis=0, keepdims=True)
    )
    part(info_ref, dx, out_ref, sent_ref)


def final_kernel(info_ref, *refs):
    inputs, refs = refs[:7], refs[7:]
    *here_refs, out_ref, sent_ref, grads_ref, dgain_ref, dkv_ref = refs
    final_rows(
        info_ref, *inputs, here_refs, out_ref, sent_ref, dgain_ref, grads_ref, dkv_ref
    )


def final_packed_kernel(info_ref, *refs):
    inputs, refs = refs[:7], refs[7:]
    *here_refs, out_ref, sent_ref, keep_ref, send_ref = refs[:-7]
    dgain_ref, acc_ref, dkv_ref, flat_ref, tmp_ref, block_ref, pair_ref = refs[-7:]
    width = inputs[2].shape[1]
    devices = 2 * keep_ref.shape[0]
    places, gain_row = early_places(width, devices)
    share = width // devices
    core = info_ref[1] % 2
    final_rows(info_ref, *inputs, here_refs, out_ref, sent_ref, dgain_ref, acc_ref, dkv_ref)

    @pl.when(pl.program_id(0) == pl.num_programs(0) - 1)
    def _():
        dgain = jnp.broadcast_to(dgain_ref[...], (width, 128)).T[0:1]
        for which, (columns, left, _, _) in enumerate(places):
            flatten(acc_ref, tmp_ref, flat_ref.at[which], width, columns, left)
        block_ref[...] = jnp.zeros(block_ref.shape, jnp.float32)
        for d in range(devices):
            for which, (_, _, start, count) in enumerate(places):
                block_ref[start : start + count, :] = flat_ref[
                    which, d * count : (d + 1) * count, :
                ]
            block_ref[gain_row : gain_row + 1, :share] = dgain[:, d * share : (d + 1) * share]
            pair_ref[d % 2, d // 2] = block_ref[...].astype(jnp.bfloat16)
        keep_ref[...] = pair_ref[core]
        send_ref[...] = pair_ref[1 - core]


def struct(shape, dtype):
    return jax.ShapeDtypeStruct(shape, dtype)


def per_seq(*shape):
    return pl.BlockSpec((1, *shape), lambda s, *_: (s,) + (0,) * len(shape))


def own_seq(*shape):
    return pl.BlockSpec((1, *shape), lambda s, info: (info[3] + s,) + (0,) * len(shape))


def call(kernel, name, micros, grid, in_specs, out_specs, out_shape, scratch, info, *operands):
    return pl.pallas_call(
        kernel,
        grid_spec=pltpu.PrefetchScalarGridSpec(
            num_scalar_prefetch=1,
            grid=grid,
            in_specs=in_specs,
            out_specs=out_specs,
            scratch_shapes=scratch,
        ),
        out_shape=out_shape,
        compiler_params=params(len(grid)),
        cost_estimate=cost(micros),
        name=name,
    )(info, *operands)


def project(info, tokens, came, weights, cosine, sine, order=None):
    seqs, width, span = came.shape
    rows = 2 * span
    all_columns = width + 2 * KVD
    in_specs = [own_seq(width, span), per_seq(width, span)]
    in_specs += [whole(array.shape) for array in weights + (cosine, sine)]
    out_specs = [per_seq(width, rows), per_seq(2, KVH, HD, rows), whole((width, all_columns))]
    out_shape = [
        struct((seqs, width, rows), jnp.bfloat16),
        struct((seqs, 2, KVH, HD, rows), jnp.bfloat16),
        struct((width, all_columns), jnp.bfloat16),
    ]
    scratch = [pltpu.VMEM((all_columns, width), jnp.bfloat16)]
    kernel = project_kernel
    if order:
        kernel = functools.partial(project_packed_kernel, order)
        out_specs.append(whole((width, 8)))
        out_shape.append(struct((width, 8), jnp.float32))
        scratch += [
            pltpu.VMEM((width * width // 128, 128), jnp.float32),
            pltpu.VMEM((width, 128), jnp.float32),
            pltpu.VMEM((8, width), jnp.float32),
        ]
    return call(
        kernel, "project", 7, (seqs,), in_specs, out_specs, out_shape, scratch,
        info, tokens, came, *weights, cosine, sine,
    )


def per_group(rows):
    heads = pl.BlockSpec((1, GROUP * HD, rows), lambda s, g: (s, g, 0))
    pairs = pl.BlockSpec((1, 2, 1, HD, rows), lambda s, g: (s, 0, g, 0, 0))
    stats = pl.BlockSpec((1, 1, 8, rows), lambda s, g: (s, g, 0, 0))
    kind = pl.BlockSpec(memory_space=pltpu.SMEM)
    return heads, pairs, stats, kind


def attend(kind, queries, pairs, other):
    seqs, width, rows = queries.shape
    heads, kv, stats, smem = per_group(rows)
    area = (5 * rows // 2, GROUP * rows // 2)
    weights = pl.BlockSpec((1, 1) + area, lambda s, g: (s, g, 0, 0))
    return pl.pallas_call(
        attend_kernel,
        grid=(seqs, KVH),
        in_specs=[smem, heads, kv, kv],
        out_specs=[heads, stats, weights],
        out_shape=[
            struct(queries.shape, jnp.bfloat16),
            struct((seqs, KVH, 8, rows), jnp.float32),
            struct((seqs, KVH) + area, jnp.bfloat16),
        ],
        compiler_params=params(2),
        cost_estimate=cost(18),
        name="attend",
    )(kind, queries, pairs, other)


def attend_back(seq, kind, queries, pairs, other, grads, inverse, scores, cosine, sine, before):
    seqs, width, rows = queries.shape
    heads = pl.BlockSpec((1, GROUP * HD, rows), lambda g: (seq, g, 0))
    kv = pl.BlockSpec((1, 2, 1, HD, rows), lambda g: (seq, 0, g, 0, 0))
    away = pl.BlockSpec((1, 2, 1, HD, rows), lambda g: (0, 0, g, 0, 0))
    stats = pl.BlockSpec((1, 1, 8, rows), lambda g: (seq, g, 0, 0))
    smem = pl.BlockSpec(memory_space=pltpu.SMEM)
    area = scores.shape[2:]
    weights = pl.BlockSpec((1, 1) + area, lambda g: (seq, g, 0, 0))
    operands = (kind, queries, pairs, other, grads, inverse, scores, cosine, sine) + tuple(before)
    kernel = attend_back_kernel
    if before:
        def kernel(*refs):
            attend_back_kernel(*refs[:9], *refs[9 + len(before) :])

    return pl.pallas_call(
        kernel,
        grid=(KVH,),
        in_specs=[smem, heads, kv, kv, heads, stats, weights]
        + [whole((HD // 2, 2 * rows)), whole((HD // 2, 2 * rows))]
        + [pl.BlockSpec(memory_space=pl.ANY)] * len(before),
        out_specs=[heads, kv, away],
        out_shape=[
            struct(queries.shape, jnp.bfloat16),
            struct(pairs.shape, jnp.float32),
            struct((1,) + pairs.shape[1:], jnp.bfloat16),
        ],
        input_output_aliases={9 + i: i for i in range(len(before))},
        scratch_shapes=[
            pltpu.VMEM((2 * rows, HD), jnp.float32),
            pltpu.VMEM((2 * rows, HD), jnp.float32),
        ],
        compiler_params=params(1),
        cost_estimate=cost(9),
        name="attend_back",
    )(*operands)


def mlp(info, mixed, tokens, came, cotangent, cot_came, gains, weights):
    seqs, width, span = came.shape
    rows = 2 * span
    shapes = [(width, width), (width, FF), (width, FF), (FF, width)]
    blocks = [own_seq(width, span), per_seq(width, span)]
    in_specs = [per_seq(width, rows)] + blocks + blocks + [whole(gains.shape)]
    out_specs = blocks + [per_seq(width, rows), per_seq(width, rows)]
    out_shape = [
        struct(tokens.shape, jnp.bfloat16),
        struct(came.shape, jnp.bfloat16),
        struct((seqs, width, rows), jnp.bfloat16),
        struct((seqs, width, rows), jnp.float32),
    ]
    turned = [pltpu.VMEM(shape[::-1], jnp.bfloat16) for shape in shapes]
    if len(weights) == 4:
        in_specs += [whole(shape) for shape in shapes]
        out_specs += [whole(shape) for shape in shapes] + [whole((width, 1))]
        out_shape += [struct(shape, jnp.float32) for shape in shapes]
        out_shape.append(struct((width, 1), jnp.float32))
        kernel, scratch = mlp_kernel, turned
    else:
        devices, height, _ = weights[0].shape
        places, _ = late_places(width, devices)
        hbm = pl.BlockSpec(memory_space=pl.ANY)
        in_specs.append(hbm)
        out_specs += [hbm, hbm]
        out_shape += [struct((devices // 2, height, 128), jnp.bfloat16)] * 2
        kernel = mlp_packed_kernel
        scratch = [pltpu.VMEM(shape, jnp.bfloat16) for shape in shapes] + turned
        scratch += [pltpu.VMEM(shape, jnp.float32) for shape in shapes]
        scratch += [
            pltpu.VMEM((width, 1), jnp.float32),
            pltpu.VMEM((width * FF // 128, 128), jnp.float32),
            pltpu.VMEM((FF, 128), jnp.float32),
            pltpu.VMEM((2, 2, devices // 2, places[2][2] - places[1][2], 128), jnp.bfloat16),
            pltpu.SemaphoreType.DMA((2, 2)),
        ]
    return call(
        kernel, "mlp", 55, (seqs,), in_specs, out_specs, out_shape, scratch,
        info, mixed, tokens, came, cotangent, cot_came, gains, *weights,
    )


def final(info, dq, own, tokens, came, dx, gains, weights, here, devices=0, height=0):
    seqs, width, span = came.shape
    rows = 2 * span
    blocks = [own_seq(width, span), per_seq(width, span)]
    in_specs = [per_seq(width, rows), per_seq(2, KVH, HD, rows)] + blocks
    in_specs += [per_seq(width, rows), whole(gains.shape), whole(weights.shape)]
    in_specs += [whole((1, 2, KVH, HD, rows))] * seqs
    out_specs, out_shape = list(blocks), [
        struct(tokens.shape, jnp.bfloat16),
        struct(came.shape, jnp.bfloat16),
    ]
    sums = [(weights.shape, jnp.float32), ((width, 1), jnp.float32)]
    scratch = [pltpu.VMEM((2, KVH, HD, rows), jnp.bfloat16)]
    if devices:
        kernel = final_packed_kernel
        out_specs += [whole((devices // 2, height, 128))] * 2
        out_shape += [struct((devices // 2, height, 128), jnp.bfloat16)] * 2
        scratch = [pltpu.VMEM(*sums[1]), pltpu.VMEM(*sums[0])] + scratch
        scratch += [
            pltpu.VMEM((3, width * width // 128, 128), jnp.float32),
            pltpu.VMEM((width, 128), jnp.float32),
            pltpu.VMEM((height, 128), jnp.float32),
            pltpu.VMEM((2, devices // 2, height, 128), jnp.bfloat16),
        ]
    else:
        kernel = final_kernel
        out_specs += [whole(shape) for shape, _ in sums]
        out_shape += [struct(*one) for one in sums]
    return call(
        kernel, "final", 13, (seqs,), in_specs, out_specs, out_shape, scratch,
        info, dq, own, tokens, came, dx, gains, weights, *here,
    )


def gather(shards, devices):
    sizes = [shard.shape[0] for shard in shards]
    joined = jnp.concatenate(shards)
    padded = -(-joined.shape[0] // 2048) * 2048
    joined = jnp.pad(joined, (0, padded - joined.shape[0])).reshape(-1, 128)
    every = lax.all_gather(joined, AXES, axis=0, tiled=True).reshape(devices, padded)
    found, start = [], 0
    for size in sizes:
        found.append(every[:, start : start + size].reshape(devices * size))
        start += size
    return found


def scatter_sum(grads, sizes, devices):
    pieces = [
        jnp.pad(grad.reshape(-1), (0, devices * size - grad.size)).reshape(devices, size)
        for grad, size in zip(grads, sizes)
    ]
    joined = jnp.concatenate(pieces, axis=1)
    total = sum(sizes)
    padded = -(-total // 2048) * 2048
    joined = jnp.pad(joined, ((0, 0), (0, padded - total))).astype(jnp.bfloat16)
    joined = joined.reshape(devices * padded // 128, 128)
    owned = lax.psum_scatter(joined, AXES, scatter_dimension=0, tiled=True)
    owned = owned.reshape(-1).astype(jnp.float32)
    found, start = [], 0
    for size in sizes:
        found.append(owned[start : start + size])
        start += size
    return found


def bit_swap(array, bit, devices):
    return lax.ppermute(array, AXES, [(i, i ^ bit) for i in range(devices)])


def doubling_order(devices):
    core, x_bit, y_bit, z_bit, *far = [1 << i for i in range(devices.bit_length() - 1)]
    return (core, y_bit, z_bit, *far, x_bit)


def gather_doubling(block, devices, sent, cross):
    core, y_bit, z_bit, *far, x_bit = doubling_order(devices)
    came = bit_swap(block[None], x_bit, devices)
    came, sent = lax.optimization_barrier((came, sent))
    crossed = cross(sent)
    held = jnp.concatenate([block[None], came])
    for bit in reversed(far):
        held = jnp.concatenate([held, bit_swap(held, bit, devices)])
    cut = block.shape[0] // 2
    upper, lower = held[:, :cut], held[:, cut:]
    upper_came = bit_swap(upper, z_bit, devices)
    lower_came = bit_swap(lower, y_bit, devices)
    upper = jnp.stack([upper, upper_came])
    lower = jnp.stack([lower, lower_came])
    upper_came = bit_swap(upper, y_bit, devices)
    lower_came = bit_swap(lower, z_bit, devices)
    upper = jnp.stack([upper, upper_came])
    lower = jnp.stack([lower, lower_came], axis=1)
    held = jnp.concatenate([upper, lower], axis=3).reshape((devices // 2,) + block.shape)
    held, crossed = lax.optimization_barrier((held, crossed))
    return jnp.concatenate([held, bit_swap(held, core, devices)]), crossed


class Halving:
    def __init__(self, keep, send, me, devices):
        self.me, self.devices = me, devices
        bits = [1 << i for i in reversed(range(devices.bit_length() - 1))]
        self.parts = [((keep,), bits[:-1])]
        self.sends, self.bits = [send], [1]

    def swap(self):
        return [bit_swap(send, bit, self.devices) for send, bit in zip(self.sends, self.bits)]

    def land(self, came):
        self.parts = [
            (arrays + (other,), bits) for (arrays, bits), other in zip(self.parts, came)
        ]

    def split(self):
        ((arrays, bits),) = self.parts
        cut = arrays[0].shape[1] // 2
        self.parts = [
            (tuple(array[:, :cut] for array in arrays), bits),
            (tuple(array[:, cut:] for array in arrays), bits),
        ]

    def merge(self):
        (upper, bits), (lower, _) = self.parts
        self.parts = [((jnp.concatenate([added(upper), added(lower)], axis=1),), bits)]

    def halve(self, *chosen):
        parts, self.sends, self.bits = [], [], list(chosen)
        for (arrays, bits), bit in zip(self.parts, chosen):
            place = bits.index(bit)
            inner = 1 << (len(bits) - 1 - place)
            side = (self.me // bit) % 2

            def pick(array, which):
                tail = array.shape[1:]
                middle = (inner,) if inner > 1 else ()
                array = array.reshape((-1, 2) + middle + tail)
                chosen_half = lax.dynamic_index_in_dim(array, which, 1, keepdims=False)
                return chosen_half.reshape((-1,) + tail)

            sent = added([pick(array, 1 - side) for array in arrays])
            self.sends.append(sent.astype(jnp.bfloat16))
            kept = added([pick(array, side) for array in arrays])
            parts.append(((kept,), bits[:place] + bits[place + 1 :]))
        self.parts = parts

    def total(self):
        return added(self.parts[0][0])[0]


def added(arrays):
    total = arrays[0].astype(jnp.float32)
    for array in arrays[1:]:
        total = total + array.astype(jnp.float32)
    return total


def body(
    tokens, cotangent, attn_gain, query_weight, key_weight, value_weight, out_weight,
    mlp_gain, gate_weight, up_weight, down_weight,
):
    seqs_here, span, width = tokens.shape
    n_seq = lax.axis_size("seq")
    devices = lax.axis_size("dp") * n_seq
    mine = lax.axis_index("seq")
    me = lax.axis_index(AXES)
    keep = seqs_here // 2
    tie = lax.optimization_barrier
    across = [(i, n_seq - 1 - i) for i in range(n_seq)]
    beside = [(i, i ^ 1) for i in range(n_seq)]
    own_low = mine < n_seq // 2
    own_start = jnp.where(own_low, 0, keep)
    other_start = jnp.where(own_low, keep, 0)
    low_block = jnp.minimum(mine, n_seq - 1 - mine)
    other_low = jnp.minimum(mine ^ 1, n_seq - 1 - (mine ^ 1))
    info = jnp.stack([low_block, me, own_low, own_start]).astype(jnp.int32)

    def others(blocks):
        return lax.dynamic_slice_in_dim(blocks, other_start, keep, 0)

    def cross(blocks):
        return lax.ppermute(blocks, "seq", across)

    def restored(whole_blocks, came):
        blocks = lax.dynamic_update_slice_in_dim(whole_blocks, came, other_start, 0)
        return blocks.transpose(0, 2, 1)

    tokens = tokens.transpose(0, 2, 1)
    cotangent = cotangent.transpose(0, 2, 1)

    freqs = rope_base ** (-2.0 * jnp.arange(HD // 2).astype(jnp.float32) / HD)
    blocks = jnp.stack([n_seq - 1 - low_block, low_block, other_low, n_seq - 1 - other_low])
    positions = (blocks[:, None] * span + jnp.arange(span)[None, :]).reshape(-1)
    angles = freqs[:, None] * positions.astype(jnp.float32)[None, :]
    cosine, sine = jnp.cos(angles), jnp.sin(angles)

    def low_high(table):
        return jnp.concatenate([table[:, span : 2 * span], table[:, :span]], axis=1)

    early_shards = (key_weight, value_weight, query_weight)
    late_shards = (out_weight, gate_weight, up_weight, down_weight)
    packed = devices & (devices - 1) == 0 and devices >= 16 and width % devices == 0
    packed = packed and all(shard.shape[0] % 128 == 0 for shard in early_shards + late_shards)
    packed = packed and attn_gain.shape[0] * devices == width

    tokens_sent = others(tokens)
    if packed:
        places, gain_row = early_places(width, devices)
        height = -(-(gain_row + 2) // 16) * 16
        gains = jnp.pad(jnp.stack([attn_gain, mlp_gain]), ((0, 0), (0, 128 - attn_gain.shape[0])))
        block = jnp.concatenate([shard.reshape(-1, 128) for shard in early_shards] + [gains])
        block = jnp.pad(block, ((0, height - block.shape[0]), (0, 0)))
        early, tokens_came = gather_doubling(block, devices, tokens_sent, cross)
        late_spots, late_height = late_places(width, devices)
        tops = [spot[2] for spot in late_spots] + [late_height]
        rows = [
            jnp.pad(shard.reshape(-1, 128), ((0, after - before - spot[3]), (0, 0)))
            for shard, spot, before, after in zip(late_shards, late_spots, tops, tops[1:])
        ]
        late = lax.all_gather(jnp.concatenate(rows), AXES, axis=0, tiled=True)
        late = (late.reshape(devices, late_height, 128),)
        queries, pairs, weights, gains = project(
            info, tokens, tokens_came, (early,), low_high(cosine), low_high(sine),
            doubling_order(devices),
        )
    else:
        tokens_came = cross(tokens_sent)
        early = gather((attn_gain, mlp_gain) + early_shards, devices)
        late = gather(late_shards, devices)
        gains = [gain[:width].astype(jnp.float32) for gain in early[:2]]
        gains = jnp.pad(jnp.stack(gains, axis=1), ((0, 0), (0, 6)))
        w_key, w_value, w_query = [
            weight[: width * columns].reshape(width, columns)
            for weight, columns in zip(early[2:], (KVD, KVD, width))
        ]
        late = tuple(
            weight[: rows * columns].reshape(rows, columns)
            for weight, (rows, columns) in zip(
                late, ((width, width), (width, FF), (width, FF), (FF, width))
            )
        )
        queries, pairs, weights = project(
            info, tokens, tokens_came, (gains, w_query, w_key, w_value),
            low_high(cosine), low_high(sine),
        )

    other = lax.ppermute(pairs, "seq", beside)
    cot_sent, queries = tie((others(cotangent), queries))
    cot_came = cross(cot_sent)
    mixed, *kept = attend(info, queries, pairs, other)
    mixed, cot_came = tie((mixed, cot_came))
    out, out_sent, dmixed, dx, *late_sums = mlp(
        info, mixed, tokens, tokens_came, cotangent, cot_came, gains, late
    )
    before, here = (), []

    def back(seq):
        *found, away = attend_back(
            seq, info, queries, pairs, other, dmixed, *kept, cosine, sine, before
        )
        here.append(lax.ppermute(away, "seq", beside))
        return found

    if packed:
        x_bit, y_bit, z_bit, *far = [1 << i for i in range(1, devices.bit_length() - 1)]
        sums = Halving(*late_sums, me, devices)
        sums.sends, out_sent, dmixed = tie((sums.sends, out_sent, dmixed))
        came = sums.swap()
        out_came = cross(out_sent)
        before = back(0)
        came, before = tie((came, before))
        sums.land(came)
        sums.split()
        sums.halve(y_bit, z_bit)
        sums.sends, before = tie((sums.sends, before))
        came = sums.swap()
        for seq in range(1, keep):
            before = back(seq)
        came, before, out_came = tie((came, before, out_came))
        sums.land(came)
        sums.halve(z_bit, y_bit)
        sums.sends, before = tie((sums.sends, before))
        came = sums.swap()
        dtokens, dtokens_sent, *early_sums = final(
            info, *before, tokens, tokens_came, dx, gains, weights, here, devices, height
        )
        few = Halving(*early_sums, me, devices)
        came, few.sends, dtokens_sent = tie((came, few.sends, dtokens_sent))
        sums.land(came)
        sums.merge()
        sums.halve(x_bit)
        few.sends, sums.sends, dtokens_sent = tie((few.sends, sums.sends, dtokens_sent))
        few_came, came = few.swap(), sums.swap()
        dtokens_came = cross(dtokens_sent)
        few.land(few_came)
        few.split()
        few.halve(y_bit, z_bit)
        few_came, came = tie((few.swap(), came))
        few.land(few_came)
        few.halve(z_bit, y_bit)
        sums.land(came)
        if far:
            sums.halve(far[0])
            few.sends, sums.sends = tie((few.sends, sums.sends))
            came = sums.swap()
        few.land(few.swap())
        few.merge()
        for bit, later in zip(far, far[1:] + [0]):
            few.halve(bit)
            few_came, came = tie((few.swap(), came))
            few.land(few_came)
            sums.land(came)
            if later:
                sums.halve(later)
                came = sums.swap()
        few.halve(x_bit)
        few.land(few.swap())
        owned = sums.total()
        late_grads = [
            owned[start : start + count].reshape(-1) for _, _, start, count in late_spots
        ]
        mlp_sum = owned[late_spots[0][3], : mlp_gain.shape[0]]
        owned = few.total()
        early_grads = [
            owned[start : start + count].reshape(-1) for _, _, start, count in places
        ]
        attn_sum = owned[gain_row, : attn_gain.shape[0]]
    else:
        out_came = cross(out_sent)
        for seq in range(keep):
            before = back(seq)
        dtokens, dtokens_sent, grads, grad_gain = final(
            info, *before, tokens, tokens_came, dx, gains, weights, here
        )
        dtokens_came = cross(dtokens_sent)
        *late_grads, mlp_sum = scatter_sum(
            late_sums, [a.shape[0] for a in late_shards + (mlp_gain,)], devices
        )
        columns = (grads[:, :KVD], grads[:, KVD : 2 * KVD], grads[:, 2 * KVD :], grad_gain)
        *early_grads, attn_sum = scatter_sum(
            columns, [a.shape[0] for a in early_shards + (attn_gain,)], devices
        )
    key_sum, value_sum, query_sum = early_grads
    out_sum, gate_sum, up_sum, down_sum = late_grads
    return (
        restored(out, out_came), restored(dtokens, dtokens_came),
        attn_sum, query_sum, key_sum, value_sum,
        out_sum, mlp_sum, gate_sum, up_sum, down_sum,
    )


def solution(mesh):
    rows = P("dp", "seq", None)
    flat = P(("dp", "seq"))
    return jax.shard_map(
        body,
        mesh=mesh,
        in_specs=(rows, rows) + (flat,) * 9,
        out_specs=(rows, rows) + (flat,) * 9,
        check_vma=False,
    )
```

```python
import functools

import jax
import jax.numpy as jnp
from jax import lax
from jax.experimental import pallas as pl
from jax.experimental.pallas import tpu as pltpu
from jax.sharding import PartitionSpec as P

HEADS = 9
KVH = 3
HD = 64
FF = 1536
GROUP = HEADS // KVH
KVD = KVH * HD
FF_BLOCK = 768

epsilon = 1e-05
rope_base = 100000.0
MASKED = -1e30
VMEM_LIMIT = 60 * 1024 * 1024
AXES = ("dp", "seq")


def nn(left, right):
    return jnp.dot(left, right, preferred_element_type=jnp.float32)


def nt(left, right):
    return lax.dot_general(
        left, right, (((1,), (1,)), ((), ())), preferred_element_type=jnp.float32
    )


def tn(left, right):
    return lax.dot_general(
        left, right, (((0,), (0,)), ((), ())), preferred_element_type=jnp.float32
    )


def cost(micros):
    return pl.CostEstimate(flops=int(micros * 5e8), bytes_accessed=int(micros * 1e6), transcendentals=0)


def whole(shape):
    return pl.BlockSpec(shape, lambda *_: (0,) * len(shape), pipeline_mode=pl.Buffered(1))


def params(count):
    return pltpu.CompilerParams(
        dimension_semantics=("arbitrary",) * count, vmem_limit_bytes=VMEM_LIMIT
    )


def unflatten(flat_ref, tmp_ref, out_ref, rows, width, left_column=0):
    if width % 128 == 0:
        count = width // 128
        for j in range(count):
            piece = flat_ref[pl.ds(j, rows, stride=count), :]
            place = left_column + 128 * j
            out_ref[:, place : place + 128] = piece.astype(out_ref.dtype)
        return
    count = 2 * width // 128
    mid = count // 2
    left = lax.broadcasted_iota(jnp.int32, (rows // 2, 128), 1) < 64
    turned = [
        pltpu.roll(flat_ref[pl.ds(mid + j, rows // 2, stride=count), :], 64, 1)
        for j in range(mid + 1)
    ]
    for j in range(mid + 1):
        odd = jnp.where(left, turned[j], turned[j + 1]) if j < mid else turned[j]
        tmp_ref[pl.ds(0, rows // 2, stride=2), :] = flat_ref[pl.ds(j, rows // 2, stride=count), :]
        tmp_ref[pl.ds(1, rows // 2, stride=2), :] = odd
        size = min(128, width - 128 * j)
        place = left_column + 128 * j
        out_ref[:, place : place + size] = tmp_ref[:rows, :size].astype(out_ref.dtype)


def flatten(grad_ref, tmp_ref, flat_ref, rows, width, left_column=0):
    if width % 128 == 0:
        count = width // 128
        for j in range(count):
            flat_ref[pl.ds(j, rows, stride=count), :] = grad_ref[
                :, left_column + 128 * j : left_column + 128 * (j + 1)
            ]
        return
    count = 2 * width // 128
    mid = count // 2
    left = lax.broadcasted_iota(jnp.int32, (rows // 2, 128), 1) < 64
    before = None
    for j in range(mid + 1):
        size = min(128, width - 128 * j)
        place = left_column + 128 * j
        tmp_ref[:rows, :size] = grad_ref[:, place : place + size]
        even = tmp_ref[pl.ds(0, rows // 2, stride=2), :]
        turned = pltpu.roll(tmp_ref[pl.ds(1, rows // 2, stride=2), :], 64, 1)
        if j < mid:
            flat_ref[pl.ds(j, rows // 2, stride=count), :] = even
            if j == 0:
                first = turned
        else:
            flat_ref[pl.ds(mid, rows // 2, stride=count), :] = jnp.where(left, even, first)
        if j:
            flat_ref[pl.ds(mid + j, rows // 2, stride=count), :] = jnp.where(left, before, turned)
        before = turned


def join(info_ref, own_ref, came_ref):
    own_low = info_ref[2] == 1
    own, came = own_ref[0].astype(jnp.float32), came_ref[0].astype(jnp.float32)
    low = jnp.where(own_low, own, came)
    high = jnp.where(own_low, came, own)
    return jnp.concatenate([low, high], axis=1)


def part(info_ref, values, own_ref, sent_ref):
    span = own_ref.shape[-1]
    own_low = info_ref[2] == 1
    low, high = values[:, :span], values[:, span:]
    own_ref[0] = jnp.where(own_low, low, high).astype(own_ref.dtype)
    sent_ref[0] = jnp.where(own_low, high, low).astype(sent_ref.dtype)


def normalise(x):
    inverse = lax.rsqrt(jnp.mean(x * x, axis=0, keepdims=True) + epsilon)
    return inverse, x * inverse


def project_rows(x, gain, wt_ref, cos_ref, sin_ref, q_ref, kv_ref):
    _, normed_f = normalise(x)
    out = nn(wt_ref[...], (normed_f * gain).astype(jnp.bfloat16))
    cosine, sine = cos_ref[...], sin_ref[...]
    half = HD // 2
    for head in range(HEADS + KVH):
        start = head * HD if head < KVH else 2 * KVD + (head - KVH) * HD
        a = out[start : start + half]
        b = out[start + half : start + HD]
        first = (a * cosine - b * sine).astype(jnp.bfloat16)
        second = (b * cosine + a * sine).astype(jnp.bfloat16)
        if head < KVH:
            kv_ref[0, 0, head, :half, :] = first
            kv_ref[0, 0, head, half:, :] = second
        else:
            spot = (head - KVH) * HD
            q_ref[0, spot : spot + half, :] = first
            q_ref[0, spot + half : spot + HD, :] = second
    for head in range(KVH):
        start = KVD + head * HD
        kv_ref[0, 1, head] = out[start : start + HD].astype(jnp.bfloat16)


def project_kernel(
    info_ref, own_ref, came_ref, gains_ref, wq_ref, wk_ref, wv_ref, cos_ref, sin_ref,
    q_ref, kv_ref, weights_ref, wt_ref,
):
    @pl.when(pl.program_id(0) == 0)
    def _():
        weights_ref[:, :KVD] = wk_ref[...]
        weights_ref[:, KVD : 2 * KVD] = wv_ref[...]
        weights_ref[:, 2 * KVD :] = wq_ref[...]
        wt_ref[...] = weights_ref[...].T

    x = join(info_ref, own_ref, came_ref)
    project_rows(x, gains_ref[:, 0:1], wt_ref, cos_ref, sin_ref, q_ref, kv_ref)


def early_places(width, devices):
    places, start = [], 0
    for columns, left in ((KVD, 0), (KVD, KVD), (width, 2 * KVD)):
        count = width * columns // 128 // devices
        places.append((columns, left, start, count))
        start += count
    return places, start


def project_packed_kernel(
    order, info_ref, own_ref, came_ref, packed_ref, cos_ref, sin_ref,
    q_ref, kv_ref, weights_ref, gains_ref, wt_ref, flat_ref, tmp_ref, row_ref,
):
    width = own_ref.shape[1]
    devices = packed_ref.shape[0]
    places, gain_row = early_places(width, devices)
    share = width // devices

    @pl.when(pl.program_id(0) == 0)
    def _():
        spots = []
        for d in range(devices):
            away = d ^ info_ref[1]
            spot = 0
            for bit in order:
                spot = spot * 2 + (away // bit) % 2
            spots.append(spot)
        for columns, left, start, count in places:
            for d in range(devices):
                flat_ref[d * count : (d + 1) * count, :] = packed_ref[
                    spots[d], start : start + count, :
                ].astype(jnp.float32)
            unflatten(flat_ref, tmp_ref, weights_ref, width, columns, left)
        wt_ref[...] = weights_ref[...].T
        row_ref[...] = jnp.zeros(row_ref.shape, jnp.float32)
        for d in range(devices):
            row_ref[0:2, d * share : (d + 1) * share] = packed_ref[
                spots[d], gain_row : gain_row + 2, :share
            ].astype(jnp.float32)
        gains_ref[...] = row_ref[...].T

    x = join(info_ref, own_ref, came_ref)
    project_rows(x, gains_ref[:, 0:1], wt_ref, cos_ref, sin_ref, q_ref, kv_ref)


def gather_keys(own, other, span):
    return jnp.concatenate([own[:, span:], own[:, :span], other], axis=1)


def stack_heads(ref, offset, span):
    return jnp.concatenate(
        [ref[0, h * HD : (h + 1) * HD, offset : offset + span] for h in range(GROUP)], axis=1
    )


def causal_mask(span):
    key = lax.broadcasted_iota(jnp.int32, (span, span), 0)
    query = lax.broadcasted_iota(jnp.int32, (span, span), 1)
    return jnp.concatenate([key <= query] * GROUP, axis=1)


def parts_of(kind, span):
    if kind == 0:
        return ((span, 0, 4 * span), (0, span, span))
    return ((span, 0, 3 * span), (0, span, 2 * span))


def masked_scores(keys, queries, mask, span):
    scores = nn(keys, queries)
    top = jnp.where(mask, scores[:span], MASKED)
    if keys.shape[0] == span:
        return top
    return jnp.concatenate([top, scores[span:]], axis=0)


def attend_kernel(kind_ref, q_ref, kv_ref, other_ref, o_ref, inverse_ref, weights_ref):
    span = q_ref.shape[-1] // 2
    keys = gather_keys(kv_ref[0, 0, 0], other_ref[0, 0, 0], span).T
    values_t = gather_keys(kv_ref[0, 1, 0], other_ref[0, 1, 0], span)
    mask = causal_mask(span)

    def run(kind):
        top = 0
        for offset, start, count in parts_of(kind, span):
            queries = stack_heads(q_ref, offset, span) * HD ** (-0.5)
            scores = masked_scores(keys[start : start + count], queries, mask, span)
            biggest = jnp.max(scores, axis=0, keepdims=True)
            weights = jnp.exp(scores - biggest)
            inverse = 1.0 / jnp.sum(weights, axis=0, keepdims=True)
            weights = weights.astype(jnp.bfloat16)
            weights_ref[0, 0, top : top + count, :] = weights
            top += count
            mixed = nn(values_t[:, start : start + count], weights)
            mixed = (mixed * inverse).astype(jnp.bfloat16)
            for h in range(GROUP):
                lanes = slice(h * span, (h + 1) * span)
                o_ref[0, h * HD : (h + 1) * HD, offset : offset + span] = mixed[:, lanes]
                inverse_ref[0, 0, h : h + 1, offset : offset + span] = inverse[:, lanes]

    for kind in range(2):
        pl.when(kind_ref[0] == kind)(functools.partial(run, kind))


def attend_back_kernel(
    kind_ref, q_ref, kv_ref, other_ref, do_ref, inverse_ref, weights_ref, cos_ref, sin_ref,
    dq_ref, own_ref, away_ref, dk_ref, dv_ref,
):
    span = q_ref.shape[-1] // 2
    half = HD // 2
    scale = HD ** (-0.5)
    keys_t = gather_keys(kv_ref[0, 0, 0], other_ref[0, 0, 0], span)
    values = gather_keys(kv_ref[0, 1, 0], other_ref[0, 1, 0], span).T

    def run(kind):
        top = 0
        for index, (offset, start, count) in enumerate(parts_of(kind, span)):
            rows = slice(start, start + count)
            queries = stack_heads(q_ref, offset, span) * scale
            inverse = jnp.concatenate(
                [inverse_ref[0, 0, h : h + 1, offset : offset + span] for h in range(GROUP)],
                axis=1,
            )
            grads = stack_heads(do_ref, offset, span).astype(jnp.float32) * inverse
            grads = grads.astype(jnp.bfloat16)
            weights = weights_ref[0, 0, top : top + count, :]
            top += count
            weight_grads = nn(values[rows], grads)
            weights_f = weights.astype(jnp.float32)
            delta = jnp.sum(weight_grads * weights_f, axis=0, keepdims=True) * inverse
            score_grads = (weights_f * (weight_grads - delta)).astype(jnp.bfloat16)
            dv = nt(weights, grads)
            dk = nt(score_grads, queries)
            if index == 0:
                dk_ref[rows, :] = dk
                dv_ref[rows, :] = dv
                if count < 4 * span:
                    dk_ref[count:, :] = jnp.zeros((4 * span - count, HD), jnp.float32)
                    dv_ref[count:, :] = jnp.zeros((4 * span - count, HD), jnp.float32)
            else:
                dk_ref[rows, :] += dk
                dv_ref[rows, :] += dv
            dq = nn(keys_t[:, rows], score_grads) * scale
            place = 0 if offset else span
            cosine = cos_ref[:, place : place + span]
            sine = sin_ref[:, place : place + span]
            for h in range(GROUP):
                a = dq[:half, h * span : (h + 1) * span]
                b = dq[half:, h * span : (h + 1) * span]
                lanes = slice(offset, offset + span)
                dq_ref[0, h * HD : h * HD + half, lanes] = (a * cosine + b * sine).astype(
                    jnp.bfloat16
                )
                dq_ref[0, h * HD + half : (h + 1) * HD, lanes] = (
                    b * cosine - a * sine
                ).astype(jnp.bfloat16)

    for kind in range(2):
        pl.when(kind_ref[0] == kind)(functools.partial(run, kind))

    def put(ref, which, grads_t):
        ref[0, which, 0] = grads_t.astype(ref.dtype)

    dk_t = dk_ref[...].T
    a, b = dk_t[:half], dk_t[half:]
    cosine, sine = cos_ref[...], sin_ref[...]
    dk_t = jnp.concatenate([a * cosine + b * sine, b * cosine - a * sine], axis=0)
    dv_t = dv_ref[...].T
    for which, grads_t in ((0, dk_t), (1, dv_t)):
        put(
            own_ref,
            which,
            jnp.concatenate([grads_t[:, span : 2 * span], grads_t[:, :span]], axis=1),
        )
        put(away_ref, which, grads_t[:, 2 * span :])


def mlp_rows(
    info_ref, o_ref, own_ref, came_ref, cot_ref, cot_came_ref, gains_ref,
    wo_ref, wg_ref, wu_ref, wd_ref, wot_ref, wgt_ref, wut_ref, wdt_ref,
    out_ref, sent_ref, do_ref, dx_ref, dwo_ref, dwg_ref, dwu_ref, dwd_ref, dgain_ref,
):
    def put(ref, index, value):
        ref[index] += value

    mixed = o_ref[0]
    x1 = join(info_ref, own_ref, came_ref) + nn(wot_ref[...], mixed)
    inverse, normed_f = normalise(x1)
    gain = gains_ref[:, 1:2]
    normed = (normed_f * gain).astype(jnp.bfloat16)
    cot = join(info_ref, cot_ref, cot_came_ref).astype(jnp.bfloat16)
    result = x1
    dnormed = jnp.zeros(x1.shape, jnp.float32)
    for start in range(0, FF, FF_BLOCK):
        cols = slice(start, start + FF_BLOCK)
        gate = nn(wgt_ref[cols, :], normed)
        up = nn(wut_ref[cols, :], normed)
        sigma = jax.nn.sigmoid(gate)
        silu = gate * sigma
        hidden = (silu * up).astype(jnp.bfloat16)
        result = result + nn(wdt_ref[:, cols], hidden)
        dhidden = nn(wd_ref[cols, :], cot)
        dgate = (dhidden * up * (sigma * (1.0 + gate * (1.0 - sigma)))).astype(jnp.bfloat16)
        dup = (dhidden * silu).astype(jnp.bfloat16)
        dnormed = dnormed + nn(wg_ref[:, cols], dgate) + nn(wu_ref[:, cols], dup)
        put(dwg_ref, (slice(None), cols), nt(normed, dgate))
        put(dwu_ref, (slice(None), cols), nt(normed, dup))
        put(dwd_ref, (cols, slice(None)), nt(hidden, cot))
    part(info_ref, result, out_ref, sent_ref)
    put(dgain_ref, ..., jnp.sum(dnormed * normed_f, axis=1, keepdims=True))
    scaled = dnormed * gain
    dx = cot.astype(jnp.float32) + inverse * (
        scaled - normed_f * jnp.mean(scaled * normed_f, axis=0, keepdims=True)
    )
    dx_ref[0] = dx
    dab = dx.astype(jnp.bfloat16)
    put(dwo_ref, ..., nt(mixed, dab))
    do_ref[0] = nn(wo_ref[...], dab).astype(jnp.bfloat16)


def mlp_kernel(*refs):
    info_ref, o_ref, own_ref, came_ref, cot_ref, cot_came_ref, gains_ref, *refs = refs
    weights, refs = refs[:4], refs[4:]
    outs, turned = refs[:-4], refs[-4:]

    @pl.when(pl.program_id(0) == 0)
    def _():
        for ref, other in zip(weights, turned):
            other[...] = ref[...].T
        for ref in outs[4:]:
            ref[...] = jnp.zeros(ref.shape, jnp.float32)

    mlp_rows(
        info_ref, o_ref, own_ref, came_ref, cot_ref, cot_came_ref, gains_ref,
        *weights, *turned, *outs,
    )


def late_places(width, devices):
    places, start = [], 0
    for rows, columns in ((width, width), (width, FF), (width, FF), (FF, width)):
        count = rows * columns // 128 // devices
        places.append((rows, columns, start, count))
        start += -(-(count + 1) // 16) * 16
    return places, start


def mlp_packed_kernel(
    info_ref, o_ref, own_ref, came_ref, cot_ref, cot_came_ref, gains_ref, packed_ref,
    out_ref, sent_ref, do_ref, dx_ref, keep_ref, send_ref,
    wo_ref, wg_ref, wu_ref, wd_ref, wot_ref, wgt_ref, wut_ref, wdt_ref,
    dwo_ref, dwg_ref, dwu_ref, dwd_ref, dgain_ref, flat_ref, tmp_ref, stage_ref, sems,
):
    width = own_ref.shape[1]
    devices = packed_ref.shape[0]
    places, total = late_places(width, devices)
    tops = [place[2] for place in places] + [total]
    sizes = [after - before for before, after in zip(tops, tops[1:])]
    step = pl.program_id(0)

    half = devices // 2
    core = info_ref[1] % 2

    def arrival(i):
        return [
            pltpu.make_async_copy(
                packed_ref.at[side * half : (side + 1) * half, tops[i] : tops[i + 1], :],
                stage_ref.at[i % 2, side, :, : sizes[i], :],
                sems.at[i % 2, side],
            )
            for side in range(2)
        ]

    def departure(i):
        return [
            pltpu.make_async_copy(
                stage_ref.at[i % 2, source, :, : sizes[i], :],
                ref.at[:, tops[i] : tops[i + 1], :],
                sems.at[i % 2, side],
            )
            for side, (ref, source) in enumerate(((keep_ref, core), (send_ref, 1 - core)))
        ]

    def start(copies):
        for copy in copies:
            copy.start()

    def wait(copies):
        for copy in copies:
            copy.wait()

    @pl.when(step == 0)
    def _():
        start(arrival(0))
        start(arrival(1))
        turned = (wot_ref, wgt_ref, wut_ref, wdt_ref)
        for ref in (dwo_ref, dwg_ref, dwu_ref, dwd_ref, dgain_ref):
            ref[...] = jnp.zeros(ref.shape, jnp.float32)
        for i, (ref, (rows, columns, _, count)) in enumerate(
            zip((wo_ref, wg_ref, wu_ref, wd_ref), places)
        ):
            wait(arrival(i))
            for d in range(devices):
                flat_ref[d * count : (d + 1) * count, :] = stage_ref[
                    i % 2, d // half, d % half, :count, :
                ].astype(jnp.float32)
            if i + 2 < len(places):
                start(arrival(i + 2))
            unflatten(flat_ref, tmp_ref, ref, rows, columns)
            turned[i][...] = ref[...].T

    mlp_rows(
        info_ref, o_ref, own_ref, came_ref, cot_ref, cot_came_ref, gains_ref,
        wo_ref, wg_ref, wu_ref, wd_ref, wot_ref, wgt_ref, wut_ref, wdt_ref,
        out_ref, sent_ref, do_ref, dx_ref, dwo_ref, dwg_ref, dwu_ref, dwd_ref, dgain_ref,
    )

    @pl.when(step == pl.num_programs(0) - 1)
    def _():
        share = width // devices
        dgain = jnp.broadcast_to(dgain_ref[...], (width, 128)).T[0:1]
        for i, (ref, (rows, columns, _, count)) in enumerate(
            zip((dwo_ref, dwg_ref, dwu_ref, dwd_ref), places)
        ):
            flatten(ref, tmp_ref, flat_ref, rows, columns)
            if i >= 2:
                wait(departure(i - 2))
            for d in range(devices):
                block = flat_ref[d * count : (d + 1) * count, :]
                if i == 0:
                    tail = jnp.concatenate(
                        [
                            dgain[:, d * share : (d + 1) * share],
                            jnp.zeros((1, 128 - share), jnp.float32),
                        ],
                        axis=1,
                    )
                    block = jnp.concatenate(
                        [block, tail, jnp.zeros((sizes[0] - count - 1, 128), jnp.float32)], axis=0
                    )
                    stage_ref[i % 2, d % 2, d // 2, : sizes[0], :] = block.astype(jnp.bfloat16)
                else:
                    stage_ref[i % 2, d % 2, d // 2, :count, :] = block.astype(jnp.bfloat16)
            start(departure(i))
        wait(departure(len(places) - 2))
        wait(departure(len(places) - 1))


def final_rows(
    info_ref, dq_ref, kv_ref, own_ref, came_ref, dx_ref, gains_ref, weights_ref, here_refs,
    out_ref, sent_ref, dgain_ref, acc_ref, dkv_ref,
):
    rows = dq_ref.shape[-1]
    step = pl.program_id(0)

    @pl.when(step == 0)
    def _():
        acc_ref[...] = jnp.zeros(acc_ref.shape, jnp.float32)
        dgain_ref[...] = jnp.zeros(dgain_ref.shape, jnp.float32)

    for seq, here_ref in enumerate(here_refs):

        @pl.when(step == seq)
        def _():
            dkv_ref[...] = (kv_ref[0] + here_ref[0].astype(jnp.float32)).astype(jnp.bfloat16)

    d = jnp.concatenate([dkv_ref[...].reshape(2 * KVD, rows), dq_ref[0]], axis=0)
    inverse, normed_f = normalise(join(info_ref, own_ref, came_ref))
    gain = gains_ref[:, 0:1]
    normed = (normed_f * gain).astype(jnp.bfloat16)
    grads = nt(normed, d)
    dnormed = nn(weights_ref[...], d)
    dgain = jnp.sum(dnormed * normed_f, axis=1, keepdims=True)

    acc_ref[...] += grads
    dgain_ref[...] += dgain

    scaled = dnormed * gain
    dx = dx_ref[0] + inverse * (
        scaled - normed_f * jnp.mean(scaled * normed_f, axis=0, keepdims=True)
    )
    part(info_ref, dx, out_ref, sent_ref)


def final_kernel(info_ref, *refs):
    inputs, refs = refs[:7], refs[7:]
    *here_refs, out_ref, sent_ref, grads_ref, dgain_ref, dkv_ref = refs
    final_rows(
        info_ref, *inputs, here_refs, out_ref, sent_ref, dgain_ref, grads_ref, dkv_ref
    )


def final_packed_kernel(info_ref, *refs):
    inputs, refs = refs[:7], refs[7:]
    *here_refs, out_ref, sent_ref, keep_ref, send_ref = refs[:-7]
    dgain_ref, acc_ref, dkv_ref, flat_ref, tmp_ref, block_ref, pair_ref = refs[-7:]
    width = inputs[2].shape[1]
    devices = 2 * keep_ref.shape[0]
    places, gain_row = early_places(width, devices)
    share = width // devices
    core = info_ref[1] % 2
    final_rows(info_ref, *inputs, here_refs, out_ref, sent_ref, dgain_ref, acc_ref, dkv_ref)

    @pl.when(pl.program_id(0) == pl.num_programs(0) - 1)
    def _():
        dgain = jnp.broadcast_to(dgain_ref[...], (width, 128)).T[0:1]
        for which, (columns, left, _, _) in enumerate(places):
            flatten(acc_ref, tmp_ref, flat_ref.at[which], width, columns, left)
        block_ref[...] = jnp.zeros(block_ref.shape, jnp.float32)
        for d in range(devices):
            for which, (_, _, start, count) in enumerate(places):
                block_ref[start : start + count, :] = flat_ref[
                    which, d * count : (d + 1) * count, :
                ]
            block_ref[gain_row : gain_row + 1, :share] = dgain[:, d * share : (d + 1) * share]
            pair_ref[d % 2, d // 2] = block_ref[...].astype(jnp.bfloat16)
        keep_ref[...] = pair_ref[core]
        send_ref[...] = pair_ref[1 - core]


def struct(shape, dtype):
    return jax.ShapeDtypeStruct(shape, dtype)


def per_seq(*shape):
    return pl.BlockSpec((1, *shape), lambda s, *_: (s,) + (0,) * len(shape))


def own_seq(*shape):
    return pl.BlockSpec((1, *shape), lambda s, info: (info[3] + s,) + (0,) * len(shape))


def call(kernel, name, micros, grid, in_specs, out_specs, out_shape, scratch, info, *operands):
    return pl.pallas_call(
        kernel,
        grid_spec=pltpu.PrefetchScalarGridSpec(
            num_scalar_prefetch=1,
            grid=grid,
            in_specs=in_specs,
            out_specs=out_specs,
            scratch_shapes=scratch,
        ),
        out_shape=out_shape,
        compiler_params=params(len(grid)),
        cost_estimate=cost(micros),
        name=name,
    )(info, *operands)


def project(info, tokens, came, weights, cosine, sine, order=None):
    seqs, width, span = came.shape
    rows = 2 * span
    all_columns = width + 2 * KVD
    in_specs = [own_seq(width, span), per_seq(width, span)]
    in_specs += [whole(array.shape) for array in weights + (cosine, sine)]
    out_specs = [per_seq(width, rows), per_seq(2, KVH, HD, rows), whole((width, all_columns))]
    out_shape = [
        struct((seqs, width, rows), jnp.bfloat16),
        struct((seqs, 2, KVH, HD, rows), jnp.bfloat16),
        struct((width, all_columns), jnp.bfloat16),
    ]
    scratch = [pltpu.VMEM((all_columns, width), jnp.bfloat16)]
    kernel = project_kernel
    if order:
        kernel = functools.partial(project_packed_kernel, order)
        out_specs.append(whole((width, 8)))
        out_shape.append(struct((width, 8), jnp.float32))
        scratch += [
            pltpu.VMEM((width * width // 128, 128), jnp.float32),
            pltpu.VMEM((width, 128), jnp.float32),
            pltpu.VMEM((8, width), jnp.float32),
        ]
    return call(
        kernel, "project", 7, (seqs,), in_specs, out_specs, out_shape, scratch,
        info, tokens, came, *weights, cosine, sine,
    )


def per_group(rows):
    heads = pl.BlockSpec((1, GROUP * HD, rows), lambda s, g: (s, g, 0))
    pairs = pl.BlockSpec((1, 2, 1, HD, rows), lambda s, g: (s, 0, g, 0, 0))
    stats = pl.BlockSpec((1, 1, 8, rows), lambda s, g: (s, g, 0, 0))
    kind = pl.BlockSpec(memory_space=pltpu.SMEM)
    return heads, pairs, stats, kind


def attend(kind, queries, pairs, other):
    seqs, width, rows = queries.shape
    heads, kv, stats, smem = per_group(rows)
    area = (5 * rows // 2, GROUP * rows // 2)
    weights = pl.BlockSpec((1, 1) + area, lambda s, g: (s, g, 0, 0))
    return pl.pallas_call(
        attend_kernel,
        grid=(seqs, KVH),
        in_specs=[smem, heads, kv, kv],
        out_specs=[heads, stats, weights],
        out_shape=[
            struct(queries.shape, jnp.bfloat16),
            struct((seqs, KVH, 8, rows), jnp.float32),
            struct((seqs, KVH) + area, jnp.bfloat16),
        ],
        compiler_params=params(2),
        cost_estimate=cost(18),
        name="attend",
    )(kind, queries, pairs, other)


def attend_back(seq, kind, queries, pairs, other, grads, inverse, scores, cosine, sine, before):
    seqs, width, rows = queries.shape
    heads = pl.BlockSpec((1, GROUP * HD, rows), lambda g: (seq, g, 0))
    kv = pl.BlockSpec((1, 2, 1, HD, rows), lambda g: (seq, 0, g, 0, 0))
    away = pl.BlockSpec((1, 2, 1, HD, rows), lambda g: (0, 0, g, 0, 0))
    stats = pl.BlockSpec((1, 1, 8, rows), lambda g: (seq, g, 0, 0))
    smem = pl.BlockSpec(memory_space=pltpu.SMEM)
    area = scores.shape[2:]
    weights = pl.BlockSpec((1, 1) + area, lambda g: (seq, g, 0, 0))
    operands = (kind, queries, pairs, other, grads, inverse, scores, cosine, sine) + tuple(before)
    kernel = attend_back_kernel
    if before:
        def kernel(*refs):
            attend_back_kernel(*refs[:9], *refs[9 + len(before) :])

    return pl.pallas_call(
        kernel,
        grid=(KVH,),
        in_specs=[smem, heads, kv, kv, heads, stats, weights]
        + [whole((HD // 2, 2 * rows)), whole((HD // 2, 2 * rows))]
        + [pl.BlockSpec(memory_space=pl.ANY)] * len(before),
        out_specs=[heads, kv, away],
        out_shape=[
            struct(queries.shape, jnp.bfloat16),
            struct(pairs.shape, jnp.float32),
            struct((1,) + pairs.shape[1:], jnp.bfloat16),
        ],
        input_output_aliases={9 + i: i for i in range(len(before))},
        scratch_shapes=[
            pltpu.VMEM((2 * rows, HD), jnp.float32),
            pltpu.VMEM((2 * rows, HD), jnp.float32),
        ],
        compiler_params=params(1),
        cost_estimate=cost(9),
        name="attend_back",
    )(*operands)


def mlp(info, mixed, tokens, came, cotangent, cot_came, gains, weights):
    seqs, width, span = came.shape
    rows = 2 * span
    shapes = [(width, width), (width, FF), (width, FF), (FF, width)]
    blocks = [own_seq(width, span), per_seq(width, span)]
    in_specs = [per_seq(width, rows)] + blocks + blocks + [whole(gains.shape)]
    out_specs = blocks + [per_seq(width, rows), per_seq(width, rows)]
    out_shape = [
        struct(tokens.shape, jnp.bfloat16),
        struct(came.shape, jnp.bfloat16),
        struct((seqs, width, rows), jnp.bfloat16),
        struct((seqs, width, rows), jnp.float32),
    ]
    turned = [pltpu.VMEM(shape[::-1], jnp.bfloat16) for shape in shapes]
    if len(weights) == 4:
        in_specs += [whole(shape) for shape in shapes]
        out_specs += [whole(shape) for shape in shapes] + [whole((width, 1))]
        out_shape += [struct(shape, jnp.float32) for shape in shapes]
        out_shape.append(struct((width, 1), jnp.float32))
        kernel, scratch = mlp_kernel, turned
    else:
        devices, height, _ = weights[0].shape
        places, _ = late_places(width, devices)
        hbm = pl.BlockSpec(memory_space=pl.ANY)
        in_specs.append(hbm)
        out_specs += [hbm, hbm]
        out_shape += [struct((devices // 2, height, 128), jnp.bfloat16)] * 2
        kernel = mlp_packed_kernel
        scratch = [pltpu.VMEM(shape, jnp.bfloat16) for shape in shapes] + turned
        scratch += [pltpu.VMEM(shape, jnp.float32) for shape in shapes]
        scratch += [
            pltpu.VMEM((width, 1), jnp.float32),
            pltpu.VMEM((width * FF // 128, 128), jnp.float32),
            pltpu.VMEM((FF, 128), jnp.float32),
            pltpu.VMEM((2, 2, devices // 2, places[2][2] - places[1][2], 128), jnp.bfloat16),
            pltpu.SemaphoreType.DMA((2, 2)),
        ]
    return call(
        kernel, "mlp", 55, (seqs,), in_specs, out_specs, out_shape, scratch,
        info, mixed, tokens, came, cotangent, cot_came, gains, *weights,
    )


def final(info, dq, own, tokens, came, dx, gains, weights, here, devices=0, height=0):
    seqs, width, span = came.shape
    rows = 2 * span
    blocks = [own_seq(width, span), per_seq(width, span)]
    in_specs = [per_seq(width, rows), per_seq(2, KVH, HD, rows)] + blocks
    in_specs += [per_seq(width, rows), whole(gains.shape), whole(weights.shape)]
    in_specs += [whole((1, 2, KVH, HD, rows))] * seqs
    out_specs, out_shape = list(blocks), [
        struct(tokens.shape, jnp.bfloat16),
        struct(came.shape, jnp.bfloat16),
    ]
    sums = [(weights.shape, jnp.float32), ((width, 1), jnp.float32)]
    scratch = [pltpu.VMEM((2, KVH, HD, rows), jnp.bfloat16)]
    if devices:
        kernel = final_packed_kernel
        out_specs += [whole((devices // 2, height, 128))] * 2
        out_shape += [struct((devices // 2, height, 128), jnp.bfloat16)] * 2
        scratch = [pltpu.VMEM(*sums[1]), pltpu.VMEM(*sums[0])] + scratch
        scratch += [
            pltpu.VMEM((3, width * width // 128, 128), jnp.float32),
            pltpu.VMEM((width, 128), jnp.float32),
            pltpu.VMEM((height, 128), jnp.float32),
            pltpu.VMEM((2, devices // 2, height, 128), jnp.bfloat16),
        ]
    else:
        kernel = final_kernel
        out_specs += [whole(shape) for shape, _ in sums]
        out_shape += [struct(*one) for one in sums]
    return call(
        kernel, "final", 13, (seqs,), in_specs, out_specs, out_shape, scratch,
        info, dq, own, tokens, came, dx, gains, weights, *here,
    )


def gather(shards, devices):
    sizes = [shard.shape[0] for shard in shards]
    joined = jnp.concatenate(shards)
    padded = -(-joined.shape[0] // 2048) * 2048
    joined = jnp.pad(joined, (0, padded - joined.shape[0])).reshape(-1, 128)
    every = lax.all_gather(joined, AXES, axis=0, tiled=True).reshape(devices, padded)
    found, start = [], 0
    for size in sizes:
        found.append(every[:, start : start + size].reshape(devices * size))
        start += size
    return found


def scatter_sum(grads, sizes, devices):
    pieces = [
        jnp.pad(grad.reshape(-1), (0, devices * size - grad.size)).reshape(devices, size)
        for grad, size in zip(grads, sizes)
    ]
    joined = jnp.concatenate(pieces, axis=1)
    total = sum(sizes)
    padded = -(-total // 2048) * 2048
    joined = jnp.pad(joined, ((0, 0), (0, padded - total))).astype(jnp.bfloat16)
    joined = joined.reshape(devices * padded // 128, 128)
    owned = lax.psum_scatter(joined, AXES, scatter_dimension=0, tiled=True)
    owned = owned.reshape(-1).astype(jnp.float32)
    found, start = [], 0
    for size in sizes:
        found.append(owned[start : start + size])
        start += size
    return found


def bit_swap(array, bit, devices):
    return lax.ppermute(array, AXES, [(i, i ^ bit) for i in range(devices)])


def doubling_order(devices):
    core, x_bit, y_bit, z_bit, *far = [1 << i for i in range(devices.bit_length() - 1)]
    return (core, y_bit, z_bit, *far, x_bit)


def gather_doubling(block, devices, sent, cross):
    core, y_bit, z_bit, *far, x_bit = doubling_order(devices)
    came = bit_swap(block[None], x_bit, devices)
    came, sent = lax.optimization_barrier((came, sent))
    crossed = cross(sent)
    held = jnp.concatenate([block[None], came])
    for bit in reversed(far):
        held = jnp.concatenate([held, bit_swap(held, bit, devices)])
    cut = block.shape[0] // 2
    upper, lower = held[:, :cut], held[:, cut:]
    upper_came = bit_swap(upper, z_bit, devices)
    lower_came = bit_swap(lower, y_bit, devices)
    upper = jnp.stack([upper, upper_came])
    lower = jnp.stack([lower, lower_came])
    upper_came = bit_swap(upper, y_bit, devices)
    lower_came = bit_swap(lower, z_bit, devices)
    upper = jnp.stack([upper, upper_came])
    lower = jnp.stack([lower, lower_came], axis=1)
    held = jnp.concatenate([upper, lower], axis=3).reshape((devices // 2,) + block.shape)
    held, crossed = lax.optimization_barrier((held, crossed))
    return jnp.concatenate([held, bit_swap(held, core, devices)]), crossed


class Halving:
    def __init__(self, keep, send, me, devices):
        self.me, self.devices = me, devices
        bits = [1 << i for i in reversed(range(devices.bit_length() - 1))]
        self.parts = [((keep,), bits[:-1])]
        self.sends, self.bits = [send], [1]

    def swap(self):
        return [bit_swap(send, bit, self.devices) for send, bit in zip(self.sends, self.bits)]

    def land(self, came):
        self.parts = [
            (arrays + (other,), bits) for (arrays, bits), other in zip(self.parts, came)
        ]

    def split(self):
        ((arrays, bits),) = self.parts
        cut = arrays[0].shape[1] // 2
        self.parts = [
            (tuple(array[:, :cut] for array in arrays), bits),
            (tuple(array[:, cut:] for array in arrays), bits),
        ]

    def merge(self):
        (upper, bits), (lower, _) = self.parts
        self.parts = [((jnp.concatenate([added(upper), added(lower)], axis=1),), bits)]

    def halve(self, *chosen):
        parts, self.sends, self.bits = [], [], list(chosen)
        for (arrays, bits), bit in zip(self.parts, chosen):
            place = bits.index(bit)
            inner = 1 << (len(bits) - 1 - place)
            side = (self.me // bit) % 2

            def pick(array, which):
                tail = array.shape[1:]
                middle = (inner,) if inner > 1 else ()
                array = array.reshape((-1, 2) + middle + tail)
                chosen_half = lax.dynamic_index_in_dim(array, which, 1, keepdims=False)
                return chosen_half.reshape((-1,) + tail)

            sent = added([pick(array, 1 - side) for array in arrays])
            self.sends.append(sent.astype(jnp.bfloat16))
            kept = added([pick(array, side) for array in arrays])
            parts.append(((kept,), bits[:place] + bits[place + 1 :]))
        self.parts = parts

    def total(self):
        return added(self.parts[0][0])[0]


def added(arrays):
    total = arrays[0].astype(jnp.float32)
    for array in arrays[1:]:
        total = total + array.astype(jnp.float32)
    return total


def body(
    tokens, cotangent, attn_gain, query_weight, key_weight, value_weight, out_weight,
    mlp_gain, gate_weight, up_weight, down_weight,
):
    seqs_here, span, width = tokens.shape
    n_seq = lax.axis_size("seq")
    devices = lax.axis_size("dp") * n_seq
    mine = lax.axis_index("seq")
    me = lax.axis_index(AXES)
    keep = seqs_here // 2
    tie = lax.optimization_barrier
    across = [(i, n_seq - 1 - i) for i in range(n_seq)]
    beside = [(i, i ^ 1) for i in range(n_seq)]
    own_low = mine < n_seq // 2
    own_start = jnp.where(own_low, 0, keep)
    other_start = jnp.where(own_low, keep, 0)
    low_block = jnp.minimum(mine, n_seq - 1 - mine)
    other_low = jnp.minimum(mine ^ 1, n_seq - 1 - (mine ^ 1))
    info = jnp.stack([low_block, me, own_low, own_start]).astype(jnp.int32)

    def others(blocks):
        return lax.dynamic_slice_in_dim(blocks, other_start, keep, 0)

    def cross(blocks):
        return lax.ppermute(blocks, "seq", across)

    def restored(whole_blocks, came):
        blocks = lax.dynamic_update_slice_in_dim(whole_blocks, came, other_start, 0)
        return blocks.transpose(0, 2, 1)

    tokens = tokens.transpose(0, 2, 1)
    cotangent = cotangent.transpose(0, 2, 1)

    freqs = rope_base ** (-2.0 * jnp.arange(HD // 2).astype(jnp.float32) / HD)
    blocks = jnp.stack([n_seq - 1 - low_block, low_block, other_low, n_seq - 1 - other_low])
    positions = (blocks[:, None] * span + jnp.arange(span)[None, :]).reshape(-1)
    angles = freqs[:, None] * positions.astype(jnp.float32)[None, :]
    cosine, sine = jnp.cos(angles), jnp.sin(angles)

    def low_high(table):
        return jnp.concatenate([table[:, span : 2 * span], table[:, :span]], axis=1)

    early_shards = (key_weight, value_weight, query_weight)
    late_shards = (out_weight, gate_weight, up_weight, down_weight)
    packed = devices & (devices - 1) == 0 and devices >= 16 and width % devices == 0
    packed = packed and all(shard.shape[0] % 128 == 0 for shard in early_shards + late_shards)
    packed = packed and attn_gain.shape[0] * devices == width

    tokens_sent = others(tokens)
    if packed:
        places, gain_row = early_places(width, devices)
        height = -(-(gain_row + 2) // 16) * 16
        gains = jnp.pad(jnp.stack([attn_gain, mlp_gain]), ((0, 0), (0, 128 - attn_gain.shape[0])))
        block = jnp.concatenate([shard.reshape(-1, 128) for shard in early_shards] + [gains])
        block = jnp.pad(block, ((0, height - block.shape[0]), (0, 0)))
        early, tokens_came = gather_doubling(block, devices, tokens_sent, cross)
        late_spots, late_height = late_places(width, devices)
        tops = [spot[2] for spot in late_spots] + [late_height]
        rows = [
            jnp.pad(shard.reshape(-1, 128), ((0, after - before - spot[3]), (0, 0)))
            for shard, spot, before, after in zip(late_shards, late_spots, tops, tops[1:])
        ]
        late = lax.all_gather(jnp.concatenate(rows), AXES, axis=0, tiled=True)
        late = (late.reshape(devices, late_height, 128),)
        queries, pairs, weights, gains = project(
            info, tokens, tokens_came, (early,), low_high(cosine), low_high(sine),
            doubling_order(devices),
        )
    else:
        tokens_came = cross(tokens_sent)
        early = gather((attn_gain, mlp_gain) + early_shards, devices)
        late = gather(late_shards, devices)
        gains = [gain[:width].astype(jnp.float32) for gain in early[:2]]
        gains = jnp.pad(jnp.stack(gains, axis=1), ((0, 0), (0, 6)))
        w_key, w_value, w_query = [
            weight[: width * columns].reshape(width, columns)
            for weight, columns in zip(early[2:], (KVD, KVD, width))
        ]
        late = tuple(
            weight[: rows * columns].reshape(rows, columns)
            for weight, (rows, columns) in zip(
                late, ((width, width), (width, FF), (width, FF), (FF, width))
            )
        )
        queries, pairs, weights = project(
            info, tokens, tokens_came, (gains, w_query, w_key, w_value),
            low_high(cosine), low_high(sine),
        )

    other = lax.ppermute(pairs, "seq", beside)
    cot_sent, queries = tie((others(cotangent), queries))
    cot_came = cross(cot_sent)
    mixed, *kept = attend(info, queries, pairs, other)
    mixed, cot_came = tie((mixed, cot_came))
    out, out_sent, dmixed, dx, *late_sums = mlp(
        info, mixed, tokens, tokens_came, cotangent, cot_came, gains, late
    )
    before, here = (), []

    def back(seq):
        *found, away = attend_back(
            seq, info, queries, pairs, other, dmixed, *kept, cosine, sine, before
        )
        here.append(lax.ppermute(away, "seq", beside))
        return found

    if packed:
        x_bit, y_bit, z_bit, *far = [1 << i for i in range(1, devices.bit_length() - 1)]
        sums = Halving(*late_sums, me, devices)
        sums.sends, out_sent, dmixed = tie((sums.sends, out_sent, dmixed))
        came = sums.swap()
        out_came = cross(out_sent)
        before = back(0)
        came, before = tie((came, before))
        sums.land(came)
        sums.split()
        sums.halve(y_bit, z_bit)
        sums.sends, before = tie((sums.sends, before))
        came = sums.swap()
        for seq in range(1, keep):
            before = back(seq)
        came, before, out_came = tie((came, before, out_came))
        sums.land(came)
        sums.halve(z_bit, y_bit)
        sums.sends, before = tie((sums.sends, before))
        came = sums.swap()
        dtokens, dtokens_sent, *early_sums = final(
            info, *before, tokens, tokens_came, dx, gains, weights, here, devices, height
        )
        few = Halving(*early_sums, me, devices)
        came, few.sends, dtokens_sent = tie((came, few.sends, dtokens_sent))
        sums.land(came)
        sums.merge()
        sums.halve(x_bit)
        few.sends, sums.sends, dtokens_sent = tie((few.sends, sums.sends, dtokens_sent))
        few_came, came = few.swap(), sums.swap()
        dtokens_came = cross(dtokens_sent)
        few.land(few_came)
        few.split()
        few.halve(y_bit, z_bit)
        few_came, came = tie((few.swap(), came))
        few.land(few_came)
        few.halve(z_bit, y_bit)
        sums.land(came)
        if far:
            sums.halve(far[0])
            few.sends, sums.sends = tie((few.sends, sums.sends))
            came = sums.swap()
        few.land(few.swap())
        few.merge()
        for bit, later in zip(far, far[1:] + [0]):
            few.halve(bit)
            few_came, came = tie((few.swap(), came))
            few.land(few_came)
            sums.land(came)
            if later:
                sums.halve(later)
                came = sums.swap()
        few.halve(x_bit)
        few.land(few.swap())
        owned = sums.total()
        late_grads = [
            owned[start : start + count].reshape(-1) for _, _, start, count in late_spots
        ]
        mlp_sum = owned[late_spots[0][3], : mlp_gain.shape[0]]
        owned = few.total()
        early_grads = [
            owned[start : start + count].reshape(-1) for _, _, start, count in places
        ]
        attn_sum = owned[gain_row, : attn_gain.shape[0]]
    else:
        out_came = cross(out_sent)
        for seq in range(keep):
            before = back(seq)
        dtokens, dtokens_sent, grads, grad_gain = final(
            info, *before, tokens, tokens_came, dx, gains, weights, here
        )
        dtokens_came = cross(dtokens_sent)
        *late_grads, mlp_sum = scatter_sum(
            late_sums, [a.shape[0] for a in late_shards + (mlp_gain,)], devices
        )
        columns = (grads[:, :KVD], grads[:, KVD : 2 * KVD], grads[:, 2 * KVD :], grad_gain)
        *early_grads, attn_sum = scatter_sum(
            columns, [a.shape[0] for a in early_shards + (attn_gain,)], devices
        )
    key_sum, value_sum, query_sum = early_grads
    out_sum, gate_sum, up_sum, down_sum = late_grads
    return (
        restored(out, out_came), restored(dtokens, dtokens_came),
        attn_sum, query_sum, key_sum, value_sum,
        out_sum, mlp_sum, gate_sum, up_sum, down_sum,
    )


def solution(mesh):
    rows = P("dp", "seq", None)
    flat = P(("dp", "seq"))
    return jax.shard_map(
        body,
        mesh=mesh,
        in_specs=(rows, rows) + (flat,) * 9,
        out_specs=(rows, rows) + (flat,) * 9,
        check_vma=False,
    )
```

```python
import functools

import jax
import jax.numpy as jnp
from jax import lax
from jax.experimental import pallas as pl
from jax.experimental.pallas import tpu as pltpu
from jax.sharding import PartitionSpec as P

HEADS = 9
KVH = 3
HD = 64
FF = 1536
GROUP = HEADS // KVH
KVD = KVH * HD
FF_BLOCK = 768

epsilon = 1e-05
rope_base = 100000.0
MASKED = -1e30
VMEM_LIMIT = 60 * 1024 * 1024
AXES = ("dp", "seq")


def nn(left, right):
    return jnp.dot(left, right, preferred_element_type=jnp.float32)


def nt(left, right):
    return lax.dot_general(
        left, right, (((1,), (1,)), ((), ())), preferred_element_type=jnp.float32
    )


def tn(left, right):
    return lax.dot_general(
        left, right, (((0,), (0,)), ((), ())), preferred_element_type=jnp.float32
    )


def cost(micros):
    return pl.CostEstimate(flops=int(micros * 5e8), bytes_accessed=int(micros * 1e6), transcendentals=0)


def whole(shape):
    return pl.BlockSpec(shape, lambda *_: (0,) * len(shape), pipeline_mode=pl.Buffered(1))


def params(count):
    return pltpu.CompilerParams(
        dimension_semantics=("arbitrary",) * count, vmem_limit_bytes=VMEM_LIMIT
    )


def unflatten(flat_ref, tmp_ref, out_ref, rows, width, left_column=0):
    if width % 128 == 0:
        count = width // 128
        for j in range(count):
            piece = flat_ref[pl.ds(j, rows, stride=count), :]
            place = left_column + 128 * j
            out_ref[:, place : place + 128] = piece.astype(out_ref.dtype)
        return
    count = 2 * width // 128
    mid = count // 2
    left = lax.broadcasted_iota(jnp.int32, (rows // 2, 128), 1) < 64
    turned = [
        pltpu.roll(flat_ref[pl.ds(mid + j, rows // 2, stride=count), :], 64, 1)
        for j in range(mid + 1)
    ]
    for j in range(mid + 1):
        odd = jnp.where(left, turned[j], turned[j + 1]) if j < mid else turned[j]
        tmp_ref[pl.ds(0, rows // 2, stride=2), :] = flat_ref[pl.ds(j, rows // 2, stride=count), :]
        tmp_ref[pl.ds(1, rows // 2, stride=2), :] = odd
        size = min(128, width - 128 * j)
        place = left_column + 128 * j
        out_ref[:, place : place + size] = tmp_ref[:rows, :size].astype(out_ref.dtype)


def flatten(grad_ref, tmp_ref, flat_ref, rows, width, left_column=0):
    if width % 128 == 0:
        count = width // 128
        for j in range(count):
            flat_ref[pl.ds(j, rows, stride=count), :] = grad_ref[
                :, left_column + 128 * j : left_column + 128 * (j + 1)
            ]
        return
    count = 2 * width // 128
    mid = count // 2
    left = lax.broadcasted_iota(jnp.int32, (rows // 2, 128), 1) < 64
    before = None
    for j in range(mid + 1):
        size = min(128, width - 128 * j)
        place = left_column + 128 * j
        tmp_ref[:rows, :size] = grad_ref[:, place : place + size]
        even = tmp_ref[pl.ds(0, rows // 2, stride=2), :]
        turned = pltpu.roll(tmp_ref[pl.ds(1, rows // 2, stride=2), :], 64, 1)
        if j < mid:
            flat_ref[pl.ds(j, rows // 2, stride=count), :] = even
            if j == 0:
                first = turned
        else:
            flat_ref[pl.ds(mid, rows // 2, stride=count), :] = jnp.where(left, even, first)
        if j:
            flat_ref[pl.ds(mid + j, rows // 2, stride=count), :] = jnp.where(left, before, turned)
        before = turned


def join(info_ref, own_ref, came_ref):
    own_low = info_ref[2] == 1
    own, came = own_ref[0].astype(jnp.float32), came_ref[0].astype(jnp.float32)
    low = jnp.where(own_low, own, came)
    high = jnp.where(own_low, came, own)
    return jnp.concatenate([low, high], axis=1)


def part(info_ref, values, own_ref, sent_ref):
    span = own_ref.shape[-1]
    own_low = info_ref[2] == 1
    low, high = values[:, :span], values[:, span:]
    own_ref[0] = jnp.where(own_low, low, high).astype(own_ref.dtype)
    sent_ref[0] = jnp.where(own_low, high, low).astype(sent_ref.dtype)


def normalise(x):
    inverse = lax.rsqrt(jnp.mean(x * x, axis=0, keepdims=True) + epsilon)
    return inverse, x * inverse


def project_rows(x, gain, wt_ref, cos_ref, sin_ref, q_ref, kv_ref):
    _, normed_f = normalise(x)
    out = nn(wt_ref[...], (normed_f * gain).astype(jnp.bfloat16))
    cosine, sine = cos_ref[...], sin_ref[...]
    half = HD // 2
    for head in range(HEADS + KVH):
        start = head * HD if head < KVH else 2 * KVD + (head - KVH) * HD
        a = out[start : start + half]
        b = out[start + half : start + HD]
        first = (a * cosine - b * sine).astype(jnp.bfloat16)
        second = (b * cosine + a * sine).astype(jnp.bfloat16)
        if head < KVH:
            kv_ref[0, 0, head, :half, :] = first
            kv_ref[0, 0, head, half:, :] = second
        else:
            spot = (head - KVH) * HD
            q_ref[0, spot : spot + half, :] = first
            q_ref[0, spot + half : spot + HD, :] = second
    for head in range(KVH):
        start = KVD + head * HD
        kv_ref[0, 1, head] = out[start : start + HD].astype(jnp.bfloat16)


def project_kernel(
    info_ref, own_ref, came_ref, gains_ref, wq_ref, wk_ref, wv_ref, cos_ref, sin_ref,
    q_ref, kv_ref, weights_ref, wt_ref,
):
    @pl.when(pl.program_id(0) == 0)
    def _():
        weights_ref[:, :KVD] = wk_ref[...]
        weights_ref[:, KVD : 2 * KVD] = wv_ref[...]
        weights_ref[:, 2 * KVD :] = wq_ref[...]
        wt_ref[...] = weights_ref[...].T

    x = join(info_ref, own_ref, came_ref)
    project_rows(x, gains_ref[:, 0:1], wt_ref, cos_ref, sin_ref, q_ref, kv_ref)


def early_places(width, devices):
    places, start = [], 0
    for columns, left in ((KVD, 0), (KVD, KVD), (width, 2 * KVD)):
        count = width * columns // 128 // devices
        places.append((columns, left, start, count))
        start += count
    return places, start


def project_packed_kernel(
    order, info_ref, own_ref, came_ref, packed_ref, cos_ref, sin_ref,
    q_ref, kv_ref, weights_ref, gains_ref, wt_ref, flat_ref, tmp_ref, row_ref,
):
    width = own_ref.shape[1]
    devices = packed_ref.shape[0]
    places, gain_row = early_places(width, devices)
    share = width // devices

    @pl.when(pl.program_id(0) == 0)
    def _():
        spots = []
        for d in range(devices):
            away = d ^ info_ref[1]
            spot = 0
            for bit in order:
                spot = spot * 2 + (away // bit) % 2
            spots.append(spot)
        for columns, left, start, count in places:
            for d in range(devices):
                flat_ref[d * count : (d + 1) * count, :] = packed_ref[
                    spots[d], start : start + count, :
                ].astype(jnp.float32)
            unflatten(flat_ref, tmp_ref, weights_ref, width, columns, left)
        wt_ref[...] = weights_ref[...].T
        row_ref[...] = jnp.zeros(row_ref.shape, jnp.float32)
        for d in range(devices):
            row_ref[0:2, d * share : (d + 1) * share] = packed_ref[
                spots[d], gain_row : gain_row + 2, :share
            ].astype(jnp.float32)
        gains_ref[...] = row_ref[...].T

    x = join(info_ref, own_ref, came_ref)
    project_rows(x, gains_ref[:, 0:1], wt_ref, cos_ref, sin_ref, q_ref, kv_ref)


def gather_keys(own, other, span):
    return jnp.concatenate([own[:, span:], own[:, :span], other], axis=1)


def stack_heads(ref, offset, span):
    return jnp.concatenate(
        [ref[0, h * HD : (h + 1) * HD, offset : offset + span] for h in range(GROUP)], axis=1
    )


def causal_mask(span):
    key = lax.broadcasted_iota(jnp.int32, (span, span), 0)
    query = lax.broadcasted_iota(jnp.int32, (span, span), 1)
    return jnp.concatenate([key <= query] * GROUP, axis=1)


def parts_of(kind, span):
    if kind == 0:
        return ((span, 0, 4 * span), (0, span, span))
    return ((span, 0, 3 * span), (0, span, 2 * span))


def masked_scores(keys, queries, mask, span):
    scores = nn(keys, queries)
    top = jnp.where(mask, scores[:span], MASKED)
    if keys.shape[0] == span:
        return top
    return jnp.concatenate([top, scores[span:]], axis=0)


def attend_kernel(kind_ref, q_ref, kv_ref, other_ref, o_ref, inverse_ref, weights_ref):
    span = q_ref.shape[-1] // 2
    keys = gather_keys(kv_ref[0, 0, 0], other_ref[0, 0, 0], span).T
    values_t = gather_keys(kv_ref[0, 1, 0], other_ref[0, 1, 0], span)
    mask = causal_mask(span)

    def run(kind):
        top = 0
        for offset, start, count in parts_of(kind, span):
            queries = stack_heads(q_ref, offset, span) * HD ** (-0.5)
            scores = masked_scores(keys[start : start + count], queries, mask, span)
            biggest = jnp.max(scores, axis=0, keepdims=True)
            weights = jnp.exp(scores - biggest)
            inverse = 1.0 / jnp.sum(weights, axis=0, keepdims=True)
            weights = weights.astype(jnp.bfloat16)
            weights_ref[0, 0, top : top + count, :] = weights
            top += count
            mixed = nn(values_t[:, start : start + count], weights)
            mixed = (mixed * inverse).astype(jnp.bfloat16)
            for h in range(GROUP):
                lanes = slice(h * span, (h + 1) * span)
                o_ref[0, h * HD : (h + 1) * HD, offset : offset + span] = mixed[:, lanes]
                inverse_ref[0, 0, h : h + 1, offset : offset + span] = inverse[:, lanes]

    for kind in range(2):
        pl.when(kind_ref[0] == kind)(functools.partial(run, kind))


def attend_back_kernel(
    kind_ref, q_ref, kv_ref, other_ref, do_ref, inverse_ref, weights_ref, cos_ref, sin_ref,
    dq_ref, own_ref, away_ref, dk_ref, dv_ref,
):
    span = q_ref.shape[-1] // 2
    half = HD // 2
    scale = HD ** (-0.5)
    keys_t = gather_keys(kv_ref[0, 0, 0], other_ref[0, 0, 0], span)
    values = gather_keys(kv_ref[0, 1, 0], other_ref[0, 1, 0], span).T

    def run(kind):
        top = 0
        for index, (offset, start, count) in enumerate(parts_of(kind, span)):
            rows = slice(start, start + count)
            queries = stack_heads(q_ref, offset, span) * scale
            inverse = jnp.concatenate(
                [inverse_ref[0, 0, h : h + 1, offset : offset + span] for h in range(GROUP)],
                axis=1,
            )
            grads = stack_heads(do_ref, offset, span).astype(jnp.float32) * inverse
            grads = grads.astype(jnp.bfloat16)
            weights = weights_ref[0, 0, top : top + count, :]
            top += count
            weight_grads = nn(values[rows], grads)
            weights_f = weights.astype(jnp.float32)
            delta = jnp.sum(weight_grads * weights_f, axis=0, keepdims=True) * inverse
            score_grads = (weights_f * (weight_grads - delta)).astype(jnp.bfloat16)
            dv = nt(weights, grads)
            dk = nt(score_grads, queries)
            if index == 0:
                dk_ref[rows, :] = dk
                dv_ref[rows, :] = dv
                if count < 4 * span:
                    dk_ref[count:, :] = jnp.zeros((4 * span - count, HD), jnp.float32)
                    dv_ref[count:, :] = jnp.zeros((4 * span - count, HD), jnp.float32)
            else:
                dk_ref[rows, :] += dk
                dv_ref[rows, :] += dv
            dq = nn(keys_t[:, rows], score_grads) * scale
            place = 0 if offset else span
            cosine = cos_ref[:, place : place + span]
            sine = sin_ref[:, place : place + span]
            for h in range(GROUP):
                a = dq[:half, h * span : (h + 1) * span]
                b = dq[half:, h * span : (h + 1) * span]
                lanes = slice(offset, offset + span)
                dq_ref[0, h * HD : h * HD + half, lanes] = (a * cosine + b * sine).astype(
                    jnp.bfloat16
                )
                dq_ref[0, h * HD + half : (h + 1) * HD, lanes] = (
                    b * cosine - a * sine
                ).astype(jnp.bfloat16)

    for kind in range(2):
        pl.when(kind_ref[0] == kind)(functools.partial(run, kind))

    def put(ref, which, grads_t):
        ref[0, which, 0] = grads_t.astype(ref.dtype)

    dk_t = dk_ref[...].T
    a, b = dk_t[:half], dk_t[half:]
    cosine, sine = cos_ref[...], sin_ref[...]
    dk_t = jnp.concatenate([a * cosine + b * sine, b * cosine - a * sine], axis=0)
    dv_t = dv_ref[...].T
    for which, grads_t in ((0, dk_t), (1, dv_t)):
        put(
            own_ref,
            which,
            jnp.concatenate([grads_t[:, span : 2 * span], grads_t[:, :span]], axis=1),
        )
        put(away_ref, which, grads_t[:, 2 * span :])


def mlp_rows(
    info_ref, o_ref, own_ref, came_ref, cot_ref, cot_came_ref, gains_ref,
    wo_ref, wg_ref, wu_ref, wd_ref, wot_ref, wgt_ref, wut_ref, wdt_ref,
    out_ref, sent_ref, do_ref, dx_ref, dwo_ref, dwg_ref, dwu_ref, dwd_ref, dgain_ref,
):
    def put(ref, index, value):
        ref[index] += value

    mixed = o_ref[0]
    x1 = join(info_ref, own_ref, came_ref) + nn(wot_ref[...], mixed)
    inverse, normed_f = normalise(x1)
    gain = gains_ref[:, 1:2]
    normed = (normed_f * gain).astype(jnp.bfloat16)
    cot = join(info_ref, cot_ref, cot_came_ref).astype(jnp.bfloat16)
    result = x1
    dnormed = jnp.zeros(x1.shape, jnp.float32)
    for start in range(0, FF, FF_BLOCK):
        cols = slice(start, start + FF_BLOCK)
        gate = nn(wgt_ref[cols, :], normed)
        up = nn(wut_ref[cols, :], normed)
        sigma = jax.nn.sigmoid(gate)
        silu = gate * sigma
        hidden = (silu * up).astype(jnp.bfloat16)
        result = result + nn(wdt_ref[:, cols], hidden)
        dhidden = nn(wd_ref[cols, :], cot)
        dgate = (dhidden * up * (sigma * (1.0 + gate * (1.0 - sigma)))).astype(jnp.bfloat16)
        dup = (dhidden * silu).astype(jnp.bfloat16)
        dnormed = dnormed + nn(wg_ref[:, cols], dgate) + nn(wu_ref[:, cols], dup)
        put(dwg_ref, (slice(None), cols), nt(normed, dgate))
        put(dwu_ref, (slice(None), cols), nt(normed, dup))
        put(dwd_ref, (cols, slice(None)), nt(hidden, cot))
    part(info_ref, result, out_ref, sent_ref)
    put(dgain_ref, ..., jnp.sum(dnormed * normed_f, axis=1, keepdims=True))
    scaled = dnormed * gain
    dx = cot.astype(jnp.float32) + inverse * (
        scaled - normed_f * jnp.mean(scaled * normed_f, axis=0, keepdims=True)
    )
    dx_ref[0] = dx
    dab = dx.astype(jnp.bfloat16)
    put(dwo_ref, ..., nt(mixed, dab))
    do_ref[0] = nn(wo_ref[...], dab).astype(jnp.bfloat16)


def mlp_kernel(*refs):
    info_ref, o_ref, own_ref, came_ref, cot_ref, cot_came_ref, gains_ref, *refs = refs
    weights, refs = refs[:4], refs[4:]
    outs, turned = refs[:-4], refs[-4:]

    @pl.when(pl.program_id(0) == 0)
    def _():
        for ref, other in zip(weights, turned):
            other[...] = ref[...].T
        for ref in outs[4:]:
            ref[...] = jnp.zeros(ref.shape, jnp.float32)

    mlp_rows(
        info_ref, o_ref, own_ref, came_ref, cot_ref, cot_came_ref, gains_ref,
        *weights, *turned, *outs,
    )


def late_places(width, devices):
    places, start = [], 0
    for rows, columns in ((width, width), (width, FF), (width, FF), (FF, width)):
        count = rows * columns // 128 // devices
        places.append((rows, columns, start, count))
        start += -(-(count + 1) // 16) * 16
    return places, start


def mlp_packed_kernel(
    info_ref, o_ref, own_ref, came_ref, cot_ref, cot_came_ref, gains_ref, packed_ref,
    out_ref, sent_ref, do_ref, dx_ref, keep_ref, send_ref,
    wo_ref, wg_ref, wu_ref, wd_ref, wot_ref, wgt_ref, wut_ref, wdt_ref,
    dwo_ref, dwg_ref, dwu_ref, dwd_ref, dgain_ref, flat_ref, tmp_ref, stage_ref, sems,
):
    width = own_ref.shape[1]
    devices = packed_ref.shape[0]
    places, total = late_places(width, devices)
    tops = [place[2] for place in places] + [total]
    sizes = [after - before for before, after in zip(tops, tops[1:])]
    step = pl.program_id(0)

    half = devices // 2
    core = info_ref[1] % 2

    def arrival(i):
        return [
            pltpu.make_async_copy(
                packed_ref.at[side * half : (side + 1) * half, tops[i] : tops[i + 1], :],
                stage_ref.at[i % 2, side, :, : sizes[i], :],
                sems.at[i % 2, side],
            )
            for side in range(2)
        ]

    def departure(i):
        return [
            pltpu.make_async_copy(
                stage_ref.at[i % 2, source, :, : sizes[i], :],
                ref.at[:, tops[i] : tops[i + 1], :],
                sems.at[i % 2, side],
            )
            for side, (ref, source) in enumerate(((keep_ref, core), (send_ref, 1 - core)))
        ]

    def start(copies):
        for copy in copies:
            copy.start()

    def wait(copies):
        for copy in copies:
            copy.wait()

    @pl.when(step == 0)
    def _():
        start(arrival(0))
        start(arrival(1))
        turned = (wot_ref, wgt_ref, wut_ref, wdt_ref)
        for ref in (dwo_ref, dwg_ref, dwu_ref, dwd_ref, dgain_ref):
            ref[...] = jnp.zeros(ref.shape, jnp.float32)
        for i, (ref, (rows, columns, _, count)) in enumerate(
            zip((wo_ref, wg_ref, wu_ref, wd_ref), places)
        ):
            wait(arrival(i))
            for d in range(devices):
                flat_ref[d * count : (d + 1) * count, :] = stage_ref[
                    i % 2, d // half, d % half, :count, :
                ].astype(jnp.float32)
            if i + 2 < len(places):
                start(arrival(i + 2))
            unflatten(flat_ref, tmp_ref, ref, rows, columns)
            turned[i][...] = ref[...].T

    mlp_rows(
        info_ref, o_ref, own_ref, came_ref, cot_ref, cot_came_ref, gains_ref,
        wo_ref, wg_ref, wu_ref, wd_ref, wot_ref, wgt_ref, wut_ref, wdt_ref,
        out_ref, sent_ref, do_ref, dx_ref, dwo_ref, dwg_ref, dwu_ref, dwd_ref, dgain_ref,
    )

    @pl.when(step == pl.num_programs(0) - 1)
    def _():
        share = width // devices
        dgain = jnp.broadcast_to(dgain_ref[...], (width, 128)).T[0:1]
        for i, (ref, (rows, columns, _, count)) in enumerate(
            zip((dwo_ref, dwg_ref, dwu_ref, dwd_ref), places)
        ):
            flatten(ref, tmp_ref, flat_ref, rows, columns)
            if i >= 2:
                wait(departure(i - 2))
            for d in range(devices):
                block = flat_ref[d * count : (d + 1) * count, :]
                if i == 0:
                    tail = jnp.concatenate(
                        [
                            dgain[:, d * share : (d + 1) * share],
                            jnp.zeros((1, 128 - share), jnp.float32),
                        ],
                        axis=1,
                    )
                    block = jnp.concatenate(
                        [block, tail, jnp.zeros((sizes[0] - count - 1, 128), jnp.float32)], axis=0
                    )
                    stage_ref[i % 2, d % 2, d // 2, : sizes[0], :] = block.astype(jnp.bfloat16)
                else:
                    stage_ref[i % 2, d % 2, d // 2, :count, :] = block.astype(jnp.bfloat16)
            start(departure(i))
        wait(departure(len(places) - 2))
        wait(departure(len(places) - 1))


def final_rows(
    info_ref, dq_ref, kv_ref, own_ref, came_ref, dx_ref, gains_ref, weights_ref, here_refs,
    out_ref, sent_ref, dgain_ref, acc_ref, dkv_ref,
):
    rows = dq_ref.shape[-1]
    step = pl.program_id(0)

    @pl.when(step == 0)
    def _():
        acc_ref[...] = jnp.zeros(acc_ref.shape, jnp.float32)
        dgain_ref[...] = jnp.zeros(dgain_ref.shape, jnp.float32)

    for seq, here_ref in enumerate(here_refs):

        @pl.when(step == seq)
        def _():
            dkv_ref[...] = (kv_ref[0] + here_ref[0].astype(jnp.float32)).astype(jnp.bfloat16)

    d = jnp.concatenate([dkv_ref[...].reshape(2 * KVD, rows), dq_ref[0]], axis=0)
    inverse, normed_f = normalise(join(info_ref, own_ref, came_ref))
    gain = gains_ref[:, 0:1]
    normed = (normed_f * gain).astype(jnp.bfloat16)
    grads = nt(normed, d)
    dnormed = nn(weights_ref[...], d)
    dgain = jnp.sum(dnormed * normed_f, axis=1, keepdims=True)

    acc_ref[...] += grads
    dgain_ref[...] += dgain

    scaled = dnormed * gain
    dx = dx_ref[0] + inverse * (
        scaled - normed_f * jnp.mean(scaled * normed_f, axis=0, keepdims=True)
    )
    part(info_ref, dx, out_ref, sent_ref)


def final_kernel(info_ref, *refs):
    inputs, refs = refs[:7], refs[7:]
    *here_refs, out_ref, sent_ref, grads_ref, dgain_ref, dkv_ref = refs
    final_rows(
        info_ref, *inputs, here_refs, out_ref, sent_ref, dgain_ref, grads_ref, dkv_ref
    )


def final_packed_kernel(info_ref, *refs):
    inputs, refs = refs[:7], refs[7:]
    *here_refs, out_ref, sent_ref, keep_ref, send_ref = refs[:-7]
    dgain_ref, acc_ref, dkv_ref, flat_ref, tmp_ref, block_ref, pair_ref = refs[-7:]
    width = inputs[2].shape[1]
    devices = 2 * keep_ref.shape[0]
    places, gain_row = early_places(width, devices)
    share = width // devices
    core = info_ref[1] % 2
    final_rows(info_ref, *inputs, here_refs, out_ref, sent_ref, dgain_ref, acc_ref, dkv_ref)

    @pl.when(pl.program_id(0) == pl.num_programs(0) - 1)
    def _():
        dgain = jnp.broadcast_to(dgain_ref[...], (width, 128)).T[0:1]
        for which, (columns, left, _, _) in enumerate(places):
            flatten(acc_ref, tmp_ref, flat_ref.at[which], width, columns, left)
        block_ref[...] = jnp.zeros(block_ref.shape, jnp.float32)
        for d in range(devices):
            for which, (_, _, start, count) in enumerate(places):
                block_ref[start : start + count, :] = flat_ref[
                    which, d * count : (d + 1) * count, :
                ]
            block_ref[gain_row : gain_row + 1, :share] = dgain[:, d * share : (d + 1) * share]
            pair_ref[d % 2, d // 2] = block_ref[...].astype(jnp.bfloat16)
        keep_ref[...] = pair_ref[core]
        send_ref[...] = pair_ref[1 - core]


def struct(shape, dtype):
    return jax.ShapeDtypeStruct(shape, dtype)


def per_seq(*shape):
    return pl.BlockSpec((1, *shape), lambda s, *_: (s,) + (0,) * len(shape))


def own_seq(*shape):
    return pl.BlockSpec((1, *shape), lambda s, info: (info[3] + s,) + (0,) * len(shape))


def call(kernel, name, micros, grid, in_specs, out_specs, out_shape, scratch, info, *operands):
    return pl.pallas_call(
        kernel,
        grid_spec=pltpu.PrefetchScalarGridSpec(
            num_scalar_prefetch=1,
            grid=grid,
            in_specs=in_specs,
            out_specs=out_specs,
            scratch_shapes=scratch,
        ),
        out_shape=out_shape,
        compiler_params=params(len(grid)),
        cost_estimate=cost(micros),
        name=name,
    )(info, *operands)


def project(info, tokens, came, weights, cosine, sine, order=None):
    seqs, width, span = came.shape
    rows = 2 * span
    all_columns = width + 2 * KVD
    in_specs = [own_seq(width, span), per_seq(width, span)]
    in_specs += [whole(array.shape) for array in weights + (cosine, sine)]
    out_specs = [per_seq(width, rows), per_seq(2, KVH, HD, rows), whole((width, all_columns))]
    out_shape = [
        struct((seqs, width, rows), jnp.bfloat16),
        struct((seqs, 2, KVH, HD, rows), jnp.bfloat16),
        struct((width, all_columns), jnp.bfloat16),
    ]
    scratch = [pltpu.VMEM((all_columns, width), jnp.bfloat16)]
    kernel = project_kernel
    if order:
        kernel = functools.partial(project_packed_kernel, order)
        out_specs.append(whole((width, 8)))
        out_shape.append(struct((width, 8), jnp.float32))
        scratch += [
            pltpu.VMEM((width * width // 128, 128), jnp.float32),
            pltpu.VMEM((width, 128), jnp.float32),
            pltpu.VMEM((8, width), jnp.float32),
        ]
    return call(
        kernel, "project", 7, (seqs,), in_specs, out_specs, out_shape, scratch,
        info, tokens, came, *weights, cosine, sine,
    )


def per_group(rows):
    heads = pl.BlockSpec((1, GROUP * HD, rows), lambda s, g: (s, g, 0))
    pairs = pl.BlockSpec((1, 2, 1, HD, rows), lambda s, g: (s, 0, g, 0, 0))
    stats = pl.BlockSpec((1, 1, 8, rows), lambda s, g: (s, g, 0, 0))
    kind = pl.BlockSpec(memory_space=pltpu.SMEM)
    return heads, pairs, stats, kind


def attend(kind, queries, pairs, other):
    seqs, width, rows = queries.shape
    heads, kv, stats, smem = per_group(rows)
    area = (5 * rows // 2, GROUP * rows // 2)
    weights = pl.BlockSpec((1, 1) + area, lambda s, g: (s, g, 0, 0))
    return pl.pallas_call(
        attend_kernel,
        grid=(seqs, KVH),
        in_specs=[smem, heads, kv, kv],
        out_specs=[heads, stats, weights],
        out_shape=[
            struct(queries.shape, jnp.bfloat16),
            struct((seqs, KVH, 8, rows), jnp.float32),
            struct((seqs, KVH) + area, jnp.bfloat16),
        ],
        compiler_params=params(2),
        cost_estimate=cost(18),
        name="attend",
    )(kind, queries, pairs, other)


def attend_back(seq, kind, queries, pairs, other, grads, inverse, scores, cosine, sine, before):
    seqs, width, rows = queries.shape
    heads = pl.BlockSpec((1, GROUP * HD, rows), lambda g: (seq, g, 0))
    kv = pl.BlockSpec((1, 2, 1, HD, rows), lambda g: (seq, 0, g, 0, 0))
    away = pl.BlockSpec((1, 2, 1, HD, rows), lambda g: (0, 0, g, 0, 0))
    stats = pl.BlockSpec((1, 1, 8, rows), lambda g: (seq, g, 0, 0))
    smem = pl.BlockSpec(memory_space=pltpu.SMEM)
    area = scores.shape[2:]
    weights = pl.BlockSpec((1, 1) + area, lambda g: (seq, g, 0, 0))
    operands = (kind, queries, pairs, other, grads, inverse, scores, cosine, sine) + tuple(before)
    kernel = attend_back_kernel
    if before:
        def kernel(*refs):
            attend_back_kernel(*refs[:9], *refs[9 + len(before) :])

    return pl.pallas_call(
        kernel,
        grid=(KVH,),
        in_specs=[smem, heads, kv, kv, heads, stats, weights]
        + [whole((HD // 2, 2 * rows)), whole((HD // 2, 2 * rows))]
        + [pl.BlockSpec(memory_space=pl.ANY)] * len(before),
        out_specs=[heads, kv, away],
        out_shape=[
            struct(queries.shape, jnp.bfloat16),
            struct(pairs.shape, jnp.float32),
            struct((1,) + pairs.shape[1:], jnp.bfloat16),
        ],
        input_output_aliases={9 + i: i for i in range(len(before))},
        scratch_shapes=[
            pltpu.VMEM((2 * rows, HD), jnp.float32),
            pltpu.VMEM((2 * rows, HD), jnp.float32),
        ],
        compiler_params=params(1),
        cost_estimate=cost(9),
        name="attend_back",
    )(*operands)


def mlp(info, mixed, tokens, came, cotangent, cot_came, gains, weights):
    seqs, width, span = came.shape
    rows = 2 * span
    shapes = [(width, width), (width, FF), (width, FF), (FF, width)]
    blocks = [own_seq(width, span), per_seq(width, span)]
    in_specs = [per_seq(width, rows)] + blocks + blocks + [whole(gains.shape)]
    out_specs = blocks + [per_seq(width, rows), per_seq(width, rows)]
    out_shape = [
        struct(tokens.shape, jnp.bfloat16),
        struct(came.shape, jnp.bfloat16),
        struct((seqs, width, rows), jnp.bfloat16),
        struct((seqs, width, rows), jnp.float32),
    ]
    turned = [pltpu.VMEM(shape[::-1], jnp.bfloat16) for shape in shapes]
    if len(weights) == 4:
        in_specs += [whole(shape) for shape in shapes]
        out_specs += [whole(shape) for shape in shapes] + [whole((width, 1))]
        out_shape += [struct(shape, jnp.float32) for shape in shapes]
        out_shape.append(struct((width, 1), jnp.float32))
        kernel, scratch = mlp_kernel, turned
    else:
        devices, height, _ = weights[0].shape
        places, _ = late_places(width, devices)
        hbm = pl.BlockSpec(memory_space=pl.ANY)
        in_specs.append(hbm)
        out_specs += [hbm, hbm]
        out_shape += [struct((devices // 2, height, 128), jnp.bfloat16)] * 2
        kernel = mlp_packed_kernel
        scratch = [pltpu.VMEM(shape, jnp.bfloat16) for shape in shapes] + turned
        scratch += [pltpu.VMEM(shape, jnp.float32) for shape in shapes]
        scratch += [
            pltpu.VMEM((width, 1), jnp.float32),
            pltpu.VMEM((width * FF // 128, 128), jnp.float32),
            pltpu.VMEM((FF, 128), jnp.float32),
            pltpu.VMEM((2, 2, devices // 2, places[2][2] - places[1][2], 128), jnp.bfloat16),
            pltpu.SemaphoreType.DMA((2, 2)),
        ]
    return call(
        kernel, "mlp", 55, (seqs,), in_specs, out_specs, out_shape, scratch,
        info, mixed, tokens, came, cotangent, cot_came, gains, *weights,
    )


def final(info, dq, own, tokens, came, dx, gains, weights, here, devices=0, height=0):
    seqs, width, span = came.shape
    rows = 2 * span
    blocks = [own_seq(width, span), per_seq(width, span)]
    in_specs = [per_seq(width, rows), per_seq(2, KVH, HD, rows)] + blocks
    in_specs += [per_seq(width, rows), whole(gains.shape), whole(weights.shape)]
    in_specs += [whole((1, 2, KVH, HD, rows))] * seqs
    out_specs, out_shape = list(blocks), [
        struct(tokens.shape, jnp.bfloat16),
        struct(came.shape, jnp.bfloat16),
    ]
    sums = [(weights.shape, jnp.float32), ((width, 1), jnp.float32)]
    scratch = [pltpu.VMEM((2, KVH, HD, rows), jnp.bfloat16)]
    if devices:
        kernel = final_packed_kernel
        out_specs += [whole((devices // 2, height, 128))] * 2
        out_shape += [struct((devices // 2, height, 128), jnp.bfloat16)] * 2
        scratch = [pltpu.VMEM(*sums[1]), pltpu.VMEM(*sums[0])] + scratch
        scratch += [
            pltpu.VMEM((3, width * width // 128, 128), jnp.float32),
            pltpu.VMEM((width, 128), jnp.float32),
            pltpu.VMEM((height, 128), jnp.float32),
            pltpu.VMEM((2, devices // 2, height, 128), jnp.bfloat16),
        ]
    else:
        kernel = final_kernel
        out_specs += [whole(shape) for shape, _ in sums]
        out_shape += [struct(*one) for one in sums]
    return call(
        kernel, "final", 13, (seqs,), in_specs, out_specs, out_shape, scratch,
        info, dq, own, tokens, came, dx, gains, weights, *here,
    )


def gather(shards, devices):
    sizes = [shard.shape[0] for shard in shards]
    joined = jnp.concatenate(shards)
    padded = -(-joined.shape[0] // 2048) * 2048
    joined = jnp.pad(joined, (0, padded - joined.shape[0])).reshape(-1, 128)
    every = lax.all_gather(joined, AXES, axis=0, tiled=True).reshape(devices, padded)
    found, start = [], 0
    for size in sizes:
        found.append(every[:, start : start + size].reshape(devices * size))
        start += size
    return found


def scatter_sum(grads, sizes, devices):
    pieces = [
        jnp.pad(grad.reshape(-1), (0, devices * size - grad.size)).reshape(devices, size)
        for grad, size in zip(grads, sizes)
    ]
    joined = jnp.concatenate(pieces, axis=1)
    total = sum(sizes)
    padded = -(-total // 2048) * 2048
    joined = jnp.pad(joined, ((0, 0), (0, padded - total))).astype(jnp.bfloat16)
    joined = joined.reshape(devices * padded // 128, 128)
    owned = lax.psum_scatter(joined, AXES, scatter_dimension=0, tiled=True)
    owned = owned.reshape(-1).astype(jnp.float32)
    found, start = [], 0
    for size in sizes:
        found.append(owned[start : start + size])
        start += size
    return found


def bit_swap(array, bit, devices):
    return lax.ppermute(array, AXES, [(i, i ^ bit) for i in range(devices)])


def doubling_order(devices):
    core, x_bit, y_bit, z_bit, *far = [1 << i for i in range(devices.bit_length() - 1)]
    return (core, y_bit, z_bit, *far, x_bit)


def gather_doubling(block, devices, sent, cross):
    core, y_bit, z_bit, *far, x_bit = doubling_order(devices)
    came = bit_swap(block[None], x_bit, devices)
    came, sent = lax.optimization_barrier((came, sent))
    crossed = cross(sent)
    held = jnp.concatenate([block[None], came])
    for bit in reversed(far):
        held = jnp.concatenate([held, bit_swap(held, bit, devices)])
    cut = block.shape[0] // 2
    upper, lower = held[:, :cut], held[:, cut:]
    upper_came = bit_swap(upper, z_bit, devices)
    lower_came = bit_swap(lower, y_bit, devices)
    upper = jnp.stack([upper, upper_came])
    lower = jnp.stack([lower, lower_came])
    upper_came = bit_swap(upper, y_bit, devices)
    lower_came = bit_swap(lower, z_bit, devices)
    upper = jnp.stack([upper, upper_came])
    lower = jnp.stack([lower, lower_came], axis=1)
    held = jnp.concatenate([upper, lower], axis=3).reshape((devices // 2,) + block.shape)
    held, crossed = lax.optimization_barrier((held, crossed))
    return jnp.concatenate([held, bit_swap(held, core, devices)]), crossed


class Halving:
    def __init__(self, keep, send, me, devices):
        self.me, self.devices = me, devices
        bits = [1 << i for i in reversed(range(devices.bit_length() - 1))]
        self.parts = [((keep,), bits[:-1])]
        self.sends, self.bits = [send], [1]

    def swap(self):
        return [bit_swap(send, bit, self.devices) for send, bit in zip(self.sends, self.bits)]

    def land(self, came):
        self.parts = [
            (arrays + (other,), bits) for (arrays, bits), other in zip(self.parts, came)
        ]

    def split(self):
        ((arrays, bits),) = self.parts
        cut = arrays[0].shape[1] // 2
        self.parts = [
            (tuple(array[:, :cut] for array in arrays), bits),
            (tuple(array[:, cut:] for array in arrays), bits),
        ]

    def merge(self):
        (upper, bits), (lower, _) = self.parts
        self.parts = [((jnp.concatenate([added(upper), added(lower)], axis=1),), bits)]

    def halve(self, *chosen):
        parts, self.sends, self.bits = [], [], list(chosen)
        for (arrays, bits), bit in zip(self.parts, chosen):
            place = bits.index(bit)
            inner = 1 << (len(bits) - 1 - place)
            side = (self.me // bit) % 2

            def pick(array, which):
                tail = array.shape[1:]
                middle = (inner,) if inner > 1 else ()
                array = array.reshape((-1, 2) + middle + tail)
                chosen_half = lax.dynamic_index_in_dim(array, which, 1, keepdims=False)
                return chosen_half.reshape((-1,) + tail)

            sent = added([pick(array, 1 - side) for array in arrays])
            self.sends.append(sent.astype(jnp.bfloat16))
            kept = added([pick(array, side) for array in arrays])
            parts.append(((kept,), bits[:place] + bits[place + 1 :]))
        self.parts = parts

    def total(self):
        return added(self.parts[0][0])[0]


def added(arrays):
    total = arrays[0].astype(jnp.float32)
    for array in arrays[1:]:
        total = total + array.astype(jnp.float32)
    return total


def body(
    tokens, cotangent, attn_gain, query_weight, key_weight, value_weight, out_weight,
    mlp_gain, gate_weight, up_weight, down_weight,
):
    seqs_here, span, width = tokens.shape
    n_seq = lax.axis_size("seq")
    devices = lax.axis_size("dp") * n_seq
    mine = lax.axis_index("seq")
    me = lax.axis_index(AXES)
    keep = seqs_here // 2
    tie = lax.optimization_barrier
    across = [(i, n_seq - 1 - i) for i in range(n_seq)]
    beside = [(i, i ^ 1) for i in range(n_seq)]
    own_low = mine < n_seq // 2
    own_start = jnp.where(own_low, 0, keep)
    other_start = jnp.where(own_low, keep, 0)
    low_block = jnp.minimum(mine, n_seq - 1 - mine)
    other_low = jnp.minimum(mine ^ 1, n_seq - 1 - (mine ^ 1))
    info = jnp.stack([low_block, me, own_low, own_start]).astype(jnp.int32)

    def others(blocks):
        return lax.dynamic_slice_in_dim(blocks, other_start, keep, 0)

    def cross(blocks):
        return lax.ppermute(blocks, "seq", across)

    def restored(whole_blocks, came):
        blocks = lax.dynamic_update_slice_in_dim(whole_blocks, came, other_start, 0)
        return blocks.transpose(0, 2, 1)

    tokens = tokens.transpose(0, 2, 1)
    cotangent = cotangent.transpose(0, 2, 1)

    freqs = rope_base ** (-2.0 * jnp.arange(HD // 2).astype(jnp.float32) / HD)
    blocks = jnp.stack([n_seq - 1 - low_block, low_block, other_low, n_seq - 1 - other_low])
    positions = (blocks[:, None] * span + jnp.arange(span)[None, :]).reshape(-1)
    angles = freqs[:, None] * positions.astype(jnp.float32)[None, :]
    cosine, sine = jnp.cos(angles), jnp.sin(angles)

    def low_high(table):
        return jnp.concatenate([table[:, span : 2 * span], table[:, :span]], axis=1)

    early_shards = (key_weight, value_weight, query_weight)
    late_shards = (out_weight, gate_weight, up_weight, down_weight)
    packed = devices & (devices - 1) == 0 and devices >= 16 and width % devices == 0
    packed = packed and all(shard.shape[0] % 128 == 0 for shard in early_shards + late_shards)
    packed = packed and attn_gain.shape[0] * devices == width

    tokens_sent = others(tokens)
    if packed:
        places, gain_row = early_places(width, devices)
        height = -(-(gain_row + 2) // 16) * 16
        gains = jnp.pad(jnp.stack([attn_gain, mlp_gain]), ((0, 0), (0, 128 - attn_gain.shape[0])))
        block = jnp.concatenate([shard.reshape(-1, 128) for shard in early_shards] + [gains])
        block = jnp.pad(block, ((0, height - block.shape[0]), (0, 0)))
        early, tokens_came = gather_doubling(block, devices, tokens_sent, cross)
        late_spots, late_height = late_places(width, devices)
        tops = [spot[2] for spot in late_spots] + [late_height]
        rows = [
            jnp.pad(shard.reshape(-1, 128), ((0, after - before - spot[3]), (0, 0)))
            for shard, spot, before, after in zip(late_shards, late_spots, tops, tops[1:])
        ]
        late = lax.all_gather(jnp.concatenate(rows), AXES, axis=0, tiled=True)
        late = (late.reshape(devices, late_height, 128),)
        queries, pairs, weights, gains = project(
            info, tokens, tokens_came, (early,), low_high(cosine), low_high(sine),
            doubling_order(devices),
        )
    else:
        tokens_came = cross(tokens_sent)
        early = gather((attn_gain, mlp_gain) + early_shards, devices)
        late = gather(late_shards, devices)
        gains = [gain[:width].astype(jnp.float32) for gain in early[:2]]
        gains = jnp.pad(jnp.stack(gains, axis=1), ((0, 0), (0, 6)))
        w_key, w_value, w_query = [
            weight[: width * columns].reshape(width, columns)
            for weight, columns in zip(early[2:], (KVD, KVD, width))
        ]
        late = tuple(
            weight[: rows * columns].reshape(rows, columns)
            for weight, (rows, columns) in zip(
                late, ((width, width), (width, FF), (width, FF), (FF, width))
            )
        )
        queries, pairs, weights = project(
            info, tokens, tokens_came, (gains, w_query, w_key, w_value),
            low_high(cosine), low_high(sine),
        )

    other = lax.ppermute(pairs, "seq", beside)
    cot_sent, queries = tie((others(cotangent), queries))
    cot_came = cross(cot_sent)
    mixed, *kept = attend(info, queries, pairs, other)
    mixed, cot_came = tie((mixed, cot_came))
    out, out_sent, dmixed, dx, *late_sums = mlp(
        info, mixed, tokens, tokens_came, cotangent, cot_came, gains, late
    )
    before, here = (), []

    def back(seq):
        *found, away = attend_back(
            seq, info, queries, pairs, other, dmixed, *kept, cosine, sine, before
        )
        here.append(lax.ppermute(away, "seq", beside))
        return found

    if packed:
        x_bit, y_bit, z_bit, *far = [1 << i for i in range(1, devices.bit_length() - 1)]
        sums = Halving(*late_sums, me, devices)
        sums.sends, out_sent, dmixed = tie((sums.sends, out_sent, dmixed))
        came = sums.swap()
        out_came = cross(out_sent)
        before = back(0)
        came, before = tie((came, before))
        sums.land(came)
        sums.split()
        sums.halve(x_bit, y_bit)
        sums.sends, before = tie((sums.sends, before))
        came = sums.swap()
        for seq in range(1, keep):
            before = back(seq)
        came, before, out_came = tie((came, before, out_came))
        sums.land(came)
        sums.halve(y_bit, x_bit)
        sums.sends, before = tie((sums.sends, before))
        came = sums.swap()
        dtokens, dtokens_sent, *early_sums = final(
            info, *before, tokens, tokens_came, dx, gains, weights, here, devices, height
        )
        few = Halving(*early_sums, me, devices)
        came, few.sends, dtokens_sent = tie((came, few.sends, dtokens_sent))
        sums.land(came)
        sums.merge()
        sums_bits = [z_bit, *far]
        sums.halve(sums_bits[0])
        few.sends, sums.sends, dtokens_sent = tie((few.sends, sums.sends, dtokens_sent))
        few_came, came = few.swap(), sums.swap()
        dtokens_came = cross(dtokens_sent)
        for index, bit in enumerate([y_bit, z_bit, *far, x_bit]):
            few.land(few_came)
            few.halve(bit)
            few_came = few.swap()
            if index < len(sums_bits):
                few_came, came = tie((few_came, came))
                sums.land(came)
                if index + 1 < len(sums_bits):
                    sums.halve(sums_bits[index + 1])
                    came = sums.swap()
        few.land(few_came)
        owned = sums.total()
        late_grads = [
            owned[start : start + count].reshape(-1) for _, _, start, count in late_spots
        ]
        mlp_sum = owned[late_spots[0][3], : mlp_gain.shape[0]]
        owned = few.total()
        early_grads = [
            owned[start : start + count].reshape(-1) for _, _, start, count in places
        ]
        attn_sum = owned[gain_row, : attn_gain.shape[0]]
    else:
        out_came = cross(out_sent)
        for seq in range(keep):
            before = back(seq)
        dtokens, dtokens_sent, grads, grad_gain = final(
            info, *before, tokens, tokens_came, dx, gains, weights, here
        )
        dtokens_came = cross(dtokens_sent)
        *late_grads, mlp_sum = scatter_sum(
            late_sums, [a.shape[0] for a in late_shards + (mlp_gain,)], devices
        )
        columns = (grads[:, :KVD], grads[:, KVD : 2 * KVD], grads[:, 2 * KVD :], grad_gain)
        *early_grads, attn_sum = scatter_sum(
            columns, [a.shape[0] for a in early_shards + (attn_gain,)], devices
        )
    key_sum, value_sum, query_sum = early_grads
    out_sum, gate_sum, up_sum, down_sum = late_grads
    return (
        restored(out, out_came), restored(dtokens, dtokens_came),
        attn_sum, query_sum, key_sum, value_sum,
        out_sum, mlp_sum, gate_sum, up_sum, down_sum,
    )


def solution(mesh):
    rows = P("dp", "seq", None)
    flat = P(("dp", "seq"))
    return jax.shard_map(
        body,
        mesh=mesh,
        in_specs=(rows, rows) + (flat,) * 9,
        out_specs=(rows, rows) + (flat,) * 9,
        check_vma=False,
    )
```
